512 devices in a mesh: row: 64 (over x, y, z_hi, core), col: 8 (over z_lo).
Axes of the slice: x: 4, y: 4, z: 16 (z_hi: 2, z_lo: 8; z = z_hi * 8 + z_lo), core: 2. Of those that a mesh axis runs over, the one named last changes fastest.
Arguments:
- amplitudes: float32 [192, 40, 1152], P('row', 'col'), may hold values from -3 to 3
- integrals: float32 [192, 40, 7680], P('row', 'col'), may hold values from -0.0625 to 0.0625
- residual: float32 [192, 40, 1152], P('row', 'col'), may hold values from -6 to 6
- occupied_energy: float32 [40], replicated, may hold values from -3 to -0.5
- virtual_energy: float32 [192], replicated, may hold values from 0.3 to 4
- window_start: int32 [1], replicated, may hold values from 0 to 34
Outputs:
- residual_new: float32 [192, 40, 1152], P('row', 'col')
- increment: float32 [192, 40, 1152], P('row', 'col')
The draws below stay inside these ranges and needn't reach their ends.
All inputs are finite; a program needn't handle non-finite values.
Results may differ from the reference program's by a relative error of at most 0.000053.
Values sent between devices are 32-bit elements; how exact they have to be, the bound alone decides.
No kernel may reach another device: no remote copies, remote signals or barrier semaphores. Data moves between devices by JAX's collectives and lax.ppermute only.
A program may use at most 64 MiB of HBM per device.

```python
import jax
import jax.numpy as jnp
from jax import lax

O = 40
V = 192
I_WIN = 6


def levels(key, extent, cuts, low, top_value):
    level, own = 1.0, jax.random.fold_in(key, 6)
    for position, parts in cuts:
        draws = jnp.exp(jax.random.uniform(jax.random.fold_in(own, position), (parts,), jnp.float32, low / len(cuts), top_value / len(cuts)))
        level = level * jnp.repeat(draws, extent[position] // parts).reshape([-1 if axis == position else 1 for axis in range(len(extent))])
    return level


def centred(own_key, shape, deviation, limit, cuts=(), held_as=jnp.bfloat16):
    gain = levels(own_key, shape, cuts, -0.22, 0.18) if cuts else 1.0
    entries = jax.random.normal(own_key, shape, jnp.float32) * deviation * gain
    return jnp.minimum(jnp.maximum(entries, -limit), limit).astype(held_as)


def setup_inputs(seed: int = 0) -> dict:
    arg_keys = jax.random.split(jax.random.key(seed), 7)
    amplitudes = centred(arg_keys[0], (V, O, I_WIN * V), 0.5, 3.0, ((0, 64), (1, 8)), jnp.float32)
    integrals = centred(arg_keys[1], (V, O, O * V), (O * V) ** -0.5, 0.0625, ((0, 64), (1, 8)), jnp.float32)
    residual = centred(arg_keys[2], (V, O, I_WIN * V), 1.0, 6.0, ((0, 64), (1, 8)), jnp.float32)
    occupied_energy = jnp.clip(jax.random.uniform(arg_keys[3], (O,), jnp.float32, -3.0, -0.5), -3.0, -0.5)
    virtual_energy = jnp.clip(jax.random.uniform(arg_keys[4], (V,), jnp.float32, 0.3, 4.0), 0.3, 4.0)
    window_start = jax.random.randint(arg_keys[5], (1,), 0, O - I_WIN + 1).astype(jnp.int32)
    return dict(amplitudes=amplitudes, integrals=integrals, residual=residual, occupied_energy=occupied_energy, virtual_energy=virtual_energy, window_start=window_start)


def reference(amplitudes, integrals, residual, occupied_energy, virtual_energy, window_start):
    amps = amplitudes.reshape(V, O, I_WIN, V)
    swapped = jnp.transpose(amps, (3, 1, 2, 0))
    mixed_amps = 2.0 * amps - swapped
    ints = integrals.reshape(V, O, O, V)
    cycle_term = jnp.einsum("akic,bkjc->ajib", mixed_amps, ints, precision=lax.Precision.HIGHEST, preferred_element_type=jnp.float32)
    residual_new = residual.reshape(V, O, I_WIN, V) + cycle_term
    offset = window_start[0].astype(jnp.int32)
    occupied_window = lax.dynamic_slice_in_dim(occupied_energy, offset, I_WIN)
    denominator = (virtual_energy[:, None, None, None] + virtual_energy[None, None, None, :]
                   - occupied_window[None, None, :, None] - occupied_energy[None, :, None, None])
    increment = residual_new / denominator
    return residual_new.reshape(V, O, I_WIN * V), increment.reshape(V, O, I_WIN * V)
```

```python
import functools

import jax
import jax.numpy as jnp
import ml_dtypes
import numpy as np
from jax import lax
from jax.experimental import pallas as pl
from jax.experimental.pallas import tpu as pltpu
from jax.sharding import Mesh, PartitionSpec as P

AXES = ("x", "y", "zh", "core", "col")
SIZES = (4, 4, 2, 2, 8)
F32, BF16 = jnp.float32, jnp.bfloat16
VMEM = pl.BlockSpec(memory_space=pltpu.VMEM)
SMEM = pl.BlockSpec(memory_space=pltpu.SMEM)
NT = (((1,), (1,)), ((), ()))
NN = (((1,), (0,)), ((), ()))


def one_hots():
    order = np.zeros((256, 256), np.float32)
    choose = np.zeros((256, 256), np.float32)
    for x in range(4):
        for y in range(4):
            for zh in range(2):
                for core in range(2):
                    for m in range(3):
                        v = x * 48 + y * 12 + zh * 6 + core * 3 + m
                        order[v, ((x * 4 + y) * 2 + core) * 8 + zh * 3 + m] = 1
                        choose[v, (x * 2 + core) * 24 + (y * 2 + zh) * 3 + m] = 1
    turn = np.zeros((800, 768), np.float32)
    for k in range(5):
        for yz in range(8):
            for i in range(6):
                for m in range(3):
                    turn[k * 160 + yz // 2 * 40 + yz % 2 * 18 + i * 3 + m, i * 128 + k * 24 + yz * 3 + m] = 1
    spread = np.zeros((128, 1280), np.float32)
    for x in range(4):
        for core in range(2):
            for j in range(5):
                for m in range(3):
                    spread[(x * 2 + core) * 16 + j * 3 + m, j * 256 + x * 48 + core * 3 + m] = 1
    return [a.astype(ml_dtypes.bfloat16) for a in (order, choose, turn, spread)]


def dot(a, b, dims=NN):
    return lax.dot_general(a, b, dims, preferred_element_type=F32)


def split2(v):
    high = v.astype(BF16)
    return high, (v - high.astype(F32)).astype(BF16)


def moved(v, hot):
    high = v.astype(BF16)
    rest = v - high.astype(F32)
    mid = rest.astype(BF16)
    low = (rest - mid.astype(F32)).astype(BF16)
    return (dot(low, hot) + dot(mid, hot)) + dot(high, hot)


def lanes192(ref, lead, n):
    if n % 2 == 0:
        return ref[lead, :, n * 192:n * 192 + 256]
    return pltpu.roll(ref[lead, :, n * 192 - 64:n * 192 + 192], 192, 1)


def weights_kernel(ints_ref, order_ref, out_ref, rows):
    rows[...] = jnp.zeros_like(rows)
    for k in range(5):
        for j in range(40):
            at = k * 128 + j // 5 * 16 + j % 5 * 3
            rows[at:at + 3, :] = lanes192(ints_ref, k, j)
        out_ref[k] = moved(rows[k * 128:(k + 1) * 128, :], order_ref[...])


def amps_kernel(zh_ref, own_ref, other_ref, order_ref, choose_ref, one_ref, two_ref, rows1, rows2):
    first = zh_ref[0] == 0
    rows1[...] = jnp.zeros_like(rows1)
    rows2[...] = jnp.zeros_like(rows2)
    for k in range(5):
        for i in range(6):
            own = lanes192(own_ref, k, i)
            other = lanes192(other_ref, k, i)
            for zh, v in ((0, jnp.where(first, own, other)), (1, jnp.where(first, other, own))):
                at = k * 40 + zh * 18 + i * 3
                rows1[at:at + 3, :] = v
                at = k * 48 + i * 8 + zh * 3
                rows2[at:at + 3, :] = v
    chosen = moved(rows2[...], choose_ref[...])
    lane = lax.broadcasted_iota(jnp.int32, (48, 128), 1)
    for n in range(8):
        part = jnp.zeros((48, 128), F32)
        for k in range(5):
            v = pltpu.roll(chosen[k * 48:(k + 1) * 48, :], (k * 24 - n * 24) % 256, 1)[:, :128]
            part = jnp.where((lane >= k * 24) & (lane < k * 24 + 24), v, part)
        for y in range(4):
            two_ref[(n // 2 * 4 + y) * 2 + n % 2] = part
    ordered = moved(rows1[...], order_ref[...])
    for y in range(4):
        one_ref[y] = ordered


def product_kernel(one_ref, two_ref, turn_ref, *refs):
    weights, out_ref = refs[:8], refs[8]
    two_high, two_low, mixed_high, mixed_low = refs[9:]
    for i in range(6):
        high, low = split2(two_ref[:, i * 8:(i + 1) * 8, :].reshape(256, 128))
        two_high[:, i * 128:(i + 1) * 128] = high
        two_low[:, i * 128:(i + 1) * 128] = low
    for k in range(5):
        turn = turn_ref[k * 160:(k + 1) * 160, :]
        swapped = dot(turn, two_high[...], NT) + dot(turn, two_low[...], NT)
        straight = jnp.concatenate([one_ref[y, k * 40:(k + 1) * 40, :] for y in range(4)], 0)
        high, low = split2(2.0 * straight - swapped)
        mixed_high[k] = high
        mixed_low[k] = low
    for pair in range(4):
        total = jnp.zeros((160, 256), F32)
        for k in range(5):
            w = jnp.concatenate(
                [ref[k, z * 16:(z + 1) * 16, :] for z in (2 * pair, 2 * pair + 1) for ref in weights], 0
            )
            high, low = split2(w)
            total += dot(mixed_high[k], low, NT) + dot(mixed_low[k], high, NT) + dot(mixed_high[k], high, NT)
        for yz in range(8):
            for half in range(2):
                to = (yz * 8 + 2 * pair + half) * 18
                at = yz // 2 * 40 + yz % 2 * 18
                out_ref[to:to + 18, :] = total[at:at + 18, half * 128:(half + 1) * 128]


def final_kernel(place_ref, occ_ref, va_ref, got_ref, spread_ref, vb_ref, res_ref, new_ref, inc_ref, sums, cyc, den):
    sums[...] = jnp.zeros_like(sums)
    for yz in range(8):
        total = got_ref[yz * 144:yz * 144 + 18, :]
        for z in range(1, 8):
            at = (yz * 8 + z) * 18
            total += got_ref[at:at + 18, :]
        sums[yz * 24:yz * 24 + 18, :] = total
    v = pltpu.roll(sums[...], place_ref[0] * 32, 1)
    lane = lax.broadcasted_iota(jnp.int32, v.shape, 1)
    other = jnp.where((lane & 16) == 0, pltpu.roll(v, 112, 1), pltpu.roll(v, 16, 1))
    v = jnp.where(place_ref[1] == 0, v, other)
    wide = moved(v, spread_ref[...])
    row = lax.broadcasted_iota(jnp.int32, (3, 192), 0)
    va = [va_ref[place_ref[2] + m] for m in range(3)]
    va = jnp.where(row == 0, va[0], jnp.where(row == 1, va[1], va[2]))
    base = vb_ref[...] + va
    for i in range(6):
        den[:, i * 192:(i + 1) * 192] = base - occ_ref[place_ref[4] + i]
    for j in range(5):
        total = wide[0:24, j * 256:(j + 1) * 256]
        for yz in range(1, 8):
            total += pltpu.roll(wide[yz * 24:(yz + 1) * 24, j * 256:(j + 1) * 256], yz * 6, 1)
        for i in range(6):
            cyc[:, i * 192:(i + 1) * 192] = total[i * 3:(i + 1) * 3, :192]
        new = res_ref[j] + cyc[...]
        new_ref[j] = new
        inc_ref[j] = new / (den[...] - occ_ref[place_ref[3] + j])


def call(kernel, n_smem, n_vmem, outs, scratch):
    shapes = [jax.ShapeDtypeStruct(s, F32) for s in outs]
    return pl.pallas_call(
        kernel,
        out_shape=shapes if len(shapes) > 1 else shapes[0],
        in_specs=[SMEM] * n_smem + [VMEM] * n_vmem,
        out_specs=[VMEM] * len(shapes) if len(shapes) > 1 else VMEM,
        scratch_shapes=scratch,
        compiler_params=pltpu.CompilerParams(vmem_limit_bytes=48 * 1024 * 1024),
    )


def body(amplitudes, integrals, residual, occupied_energy, virtual_energy, window_start):
    order, choose, turn, spread = [jnp.asarray(a) for a in one_hots()]
    x, y, zh, core, col = [lax.axis_index(a).astype(jnp.int32) for a in AXES]
    amps = jnp.transpose(amplitudes, (1, 0, 2))
    ints = jnp.transpose(integrals, (1, 0, 2))
    res = jnp.transpose(residual, (1, 0, 2))
    other = lax.ppermute(amps, "zh", [(0, 1), (1, 0)])
    weights = call(weights_kernel, 0, 2, [(5, 128, 256)], [pltpu.VMEM((640, 256), F32)])(ints, order)
    along = [weights] + [
        lax.ppermute(weights, "x", [(s, (s - d) % 4) for s in range(4)]) for d in (1, 2, 3)
    ]
    across = [lax.ppermute(w, "core", [(0, 1), (1, 0)]) for w in along]
    one, two = call(
        amps_kernel, 1, 4, [(4, 200, 256), (32, 48, 128)],
        [pltpu.VMEM((200, 256), F32), pltpu.VMEM((240, 256), F32)],
    )(zh.reshape(1), amps, other, order, choose)
    two = lax.all_to_all(two, ("x", "y", "core"), 0, 0, tiled=True)
    one = lax.all_to_all(one, "y", 0, 0, tiled=True)
    ordered = [w for pair in zip(along, across) for w in pair]
    partial = call(
        product_kernel, 0, 11, [(1152, 128)],
        [pltpu.VMEM((256, 768), BF16)] * 2 + [pltpu.VMEM((5, 160, 256), BF16)] * 2,
    )(one, two, turn, *ordered)
    got = lax.all_to_all(partial, ("y", "zh", "col"), 0, 0, tiled=True)
    r = ((x * 4 + y) * 2 + zh) * 2 + core
    place = jnp.stack([x, core, r * 3, col * 5, window_start[0]])
    new, inc = call(
        final_kernel, 3, 4, [(5, 3, 1152)] * 2,
        [pltpu.VMEM((192, 128), F32), pltpu.VMEM((3, 1152), F32), pltpu.VMEM((3, 1152), F32)],
    )(place, occupied_energy, virtual_energy, got, spread, virtual_energy.reshape(1, 192), res)
    return jnp.transpose(new, (1, 0, 2)), jnp.transpose(inc, (1, 0, 2))


def solution(mesh):
    fine = Mesh(mesh.devices.reshape(SIZES), AXES)
    split = P(("x", "y", "zh", "core"), "col", None)
    return jax.shard_map(
        body, mesh=fine, in_specs=(split, split, split, P(), P(), P()), out_specs=(split, split), check_vma=False
    )
```

```python
import jax
import jax.numpy as jnp
from jax import lax
from jax.experimental import pallas as pl
from jax.experimental.pallas import tpu as pltpu
from jax.sharding import Mesh, PartitionSpec as P

AXES = ("x", "y", "zh", "core", "col")
SIZES = (4, 4, 2, 2, 8)
F32, BF16 = jnp.float32, jnp.bfloat16
VMEM = pl.BlockSpec(memory_space=pltpu.VMEM)
SMEM = pl.BlockSpec(memory_space=pltpu.SMEM)
NT = (((1,), (1,)), ((), ()))
NN = (((1,), (0,)), ((), ()))


def index(shape, axis):
    return lax.broadcasted_iota(jnp.int32, shape, axis)


def third(n, count):
    return sum((n >= 3 * s).astype(jnp.int32) for s in range(1, count))


def hot(mask):
    return jnp.where(mask, 1.0, 0.0).astype(BF16)


def order_matrix():
    n = index((1, 256), 1)
    q = n & 7
    zh = third(q, 2)
    v = (n >> 6) * 48 + ((n >> 4) & 3) * 12 + zh * 6 + ((n >> 3) & 1) * 3 + q - zh * 3
    v = jnp.where(q < 6, v, -1)
    return hot(index((256, 256), 0) == v)


def choose_matrix():
    n = index((1, 256), 1)
    block = sum((n >= 24 * s).astype(jnp.int32) for s in range(1, 11))
    q = n - block * 24
    yz = third(q, 8)
    v = (block >> 1) * 48 + (block & 1) * 3 + yz * 6 + q - yz * 3
    v = jnp.where(block < 8, v, -1)
    return hot(index((256, 256), 0) == v)


def turn_matrix():
    n = index((1, 768), 1)
    i, q = n >> 7, n & 127
    k = sum((q >= 24 * s).astype(jnp.int32) for s in range(1, 6))
    q = q - k * 24
    yz = third(q, 8)
    row = k * 192 + (yz >> 1) * 48 + (i & 1) * 24 + (yz & 1) * 9 + (i >> 1) * 3 + q - yz * 3
    row = jnp.where(k < 5, row, -1)
    return hot(index((960, 768), 0) == row)


def spread_matrix():
    n = index((1, 1280), 1)
    j, q = n >> 8, n & 255
    x = sum((q >= 48 * s).astype(jnp.int32) for s in range(1, 6))
    q = q - x * 48
    core = third(q, 2)
    row = (x * 2 + core) * 16 + j * 3 + q - core * 3
    row = jnp.where((x < 4) & (q < 6), row, -1)
    return hot(index((128, 1280), 0) == row)


def dot(a, b, dims=NN):
    return lax.dot_general(a, b, dims, preferred_element_type=F32)


def split2(v):
    high = v.astype(BF16)
    return high, (v - high.astype(F32)).astype(BF16)


def moved(v, hot):
    high = v.astype(BF16)
    rest = v - high.astype(F32)
    mid = rest.astype(BF16)
    low = (rest - mid.astype(F32)).astype(BF16)
    return (dot(low, hot) + dot(mid, hot)) + dot(high, hot)


def lanes192(ref, lead, n):
    if n % 2 == 0:
        return ref[lead, :, n * 192:n * 192 + 256]
    return pltpu.roll(ref[lead, :, n * 192 - 64:n * 192 + 192], 192, 1)


def weights_kernel(ints_ref, out_ref, mark_ref):
    out_ref[...] = jnp.zeros_like(out_ref)
    mark_ref[...] = jnp.zeros_like(mark_ref)
    lane = index((3, 128), 1)
    for k in range(5):
        for j in range(20):
            at = j // 5 * 16 + j % 5 * 3
            near = lanes192(ints_ref, k, j)
            far = pltpu.roll(lanes192(ints_ref, k, j + 20), 64, 1)
            out_ref[k, at:at + 3, :128] = near[:, :128]
            out_ref[k, at:at + 3, 128:256] = jnp.where(lane < 64, near[:, 128:], far[:, :128])
            out_ref[k, at:at + 3, 256:] = far[:, 128:]


def amps_kernel(zh_ref, own_ref, other_ref, mark_ref, one_ref, two_ref, rows):
    first = zh_ref[0] == 0
    rows[...] = jnp.zeros_like(rows)
    one_ref[...] = jnp.zeros_like(one_ref)
    for k in range(5):
        for p in range(3):
            own = own_ref[k, :, p * 384:(p + 1) * 384]
            other = other_ref[k, :, p * 384:(p + 1) * 384]
            for zh, v in ((0, jnp.where(first, own, other)), (1, jnp.where(first, other, own))):
                at = k * 24 + zh * 9 + p * 3
                for y in range(4):
                    one_ref[y, at:at + 3, :] = v
                at = k * 48 + p * 16 + zh * 3
                rows[at:at + 3, :] = v[:, :256]
                rows[at + 8:at + 11, :] = pltpu.roll(v[:, 128:], 192, 1)
    chosen = moved(rows[...], choose_matrix())
    lane = index((48, 128), 1)
    for n in range(8):
        part = jnp.zeros((48, 128), F32)
        for k in range(5):
            v = pltpu.roll(chosen[k * 48:(k + 1) * 48, :], (k * 24 - n * 24) % 256, 1)[:, :128]
            part = jnp.where((lane >= k * 24) & (lane < k * 24 + 24), v, part)
        for y in range(4):
            two_ref[(n // 2 * 4 + y) * 2 + n % 2] = part


def product_kernel(one_ref, two_ref, *refs):
    weights, out_ref = refs[:8], refs[8]
    two_high, two_low, mixed_high, mixed_low = refs[9:]
    for i in range(6):
        high, low = split2(two_ref[:, i * 8:(i + 1) * 8, :].reshape(256, 128))
        two_high[:, i * 128:(i + 1) * 128] = high
        two_low[:, i * 128:(i + 1) * 128] = low
    order, turn = order_matrix(), turn_matrix()
    lane = index((24, 256), 1)
    for k in range(5):
        turn_k = turn[k * 192:(k + 1) * 192, :]
        swapped = dot(dot(turn_k, two_low[...], NT).astype(BF16), order, NT)
        swapped += dot(dot(turn_k, two_high[...], NT).astype(BF16), order, NT)
        straight = []
        for y in range(4):
            v = one_ref[y, k * 24:(k + 1) * 24, :]
            straight.append(jnp.where(lane < 192, v[:, :256], 0.0))
            straight.append(jnp.where(lane < 192, pltpu.roll(v[:, 128:], 192, 1), 0.0))
        high, low = split2(2.0 * jnp.concatenate(straight, 0) - swapped)
        mixed_high[k] = high
        mixed_low[k] = low
    for z in range(4):
        total = jnp.zeros((192, 256), F32)
        for k in range(5):
            rows = [ref[k, z * 16:(z + 1) * 16, :] for ref in weights]
            near = [v[:, :256] for v in rows]
            far = [pltpu.roll(v[:, 128:], 192, 1) for v in rows]
            high, low = split2(jnp.concatenate(near + far, 0))
            total += dot(mixed_high[k], low, NT) + dot(mixed_low[k], high, NT) + dot(mixed_high[k], high, NT)
        for yz in range(8):
            for half in range(2):
                for e in range(2):
                    to = (yz * 8 + z + 4 * half) * 18 + e * 9
                    at = yz // 2 * 48 + e * 24 + yz % 2 * 9
                    out_ref[to:to + 9, :] = total[at:at + 9, half * 128:(half + 1) * 128]


def final_kernel(place_ref, occ_ref, va_ref, got_ref, vb_ref, res_ref, new_ref, inc_ref, sums, cyc, den):
    sums[...] = jnp.zeros_like(sums)
    for yz in range(8):
        total = got_ref[yz * 144:yz * 144 + 18, :]
        for z in range(1, 8):
            at = (yz * 8 + z) * 18
            total += got_ref[at:at + 18, :]
        sums[yz * 24:yz * 24 + 18, :] = total
    v = pltpu.roll(sums[...], place_ref[0] * 32, 1)
    lane = lax.broadcasted_iota(jnp.int32, v.shape, 1)
    other = jnp.where((lane & 16) == 0, pltpu.roll(v, 112, 1), pltpu.roll(v, 16, 1))
    v = jnp.where(place_ref[1] == 0, v, other)
    wide = moved(v, spread_matrix())
    row = lax.broadcasted_iota(jnp.int32, (3, 192), 0)
    va = [va_ref[place_ref[2] + m] for m in range(3)]
    va = jnp.where(row == 0, va[0], jnp.where(row == 1, va[1], va[2]))
    base = vb_ref[...] + va
    for i in range(6):
        den[:, i * 192:(i + 1) * 192] = base - occ_ref[place_ref[4] + i]
    for j in range(5):
        total = wide[0:24, j * 256:(j + 1) * 256]
        for yz in range(1, 8):
            total += pltpu.roll(wide[yz * 24:(yz + 1) * 24, j * 256:(j + 1) * 256], yz * 6, 1)
        for i in range(6):
            cyc[:, i * 192:(i + 1) * 192] = total[i % 2 * 9 + i // 2 * 3:i % 2 * 9 + i // 2 * 3 + 3, :192]
        new = res_ref[j] + cyc[...]
        new_ref[j] = new
        inc_ref[j] = new / (den[...] - occ_ref[place_ref[3] + j])


def call(kernel, n_smem, n_vmem, outs, scratch):
    shapes = [jax.ShapeDtypeStruct(s, F32) for s in outs]
    return pl.pallas_call(
        kernel,
        out_shape=shapes if len(shapes) > 1 else shapes[0],
        in_specs=[SMEM] * n_smem + [VMEM] * n_vmem,
        out_specs=[VMEM] * len(shapes) if len(shapes) > 1 else VMEM,
        scratch_shapes=scratch,
        compiler_params=pltpu.CompilerParams(vmem_limit_bytes=48 * 1024 * 1024),
    )


def body(amplitudes, integrals, residual, occupied_energy, virtual_energy, window_start):
    x, y, zh, core, col = [lax.axis_index(a).astype(jnp.int32) for a in AXES]
    amps = jnp.transpose(amplitudes, (1, 0, 2))
    ints = jnp.transpose(integrals, (1, 0, 2))
    res = jnp.transpose(residual, (1, 0, 2))
    other = lax.ppermute(amps, "zh", [(0, 1), (1, 0)])
    weights, mark = call(weights_kernel, 0, 1, [(5, 64, 384), (8, 128)], [])(ints)
    along = [weights] + [
        lax.ppermute(weights, "x", [(s, (s - d) % 4) for s in range(4)]) for d in (1, 2, 3)
    ]
    across = [lax.ppermute(w, "core", [(0, 1), (1, 0)]) for w in along]
    one, two = call(amps_kernel, 1, 3, [(4, 120, 384), (32, 48, 128)], [pltpu.VMEM((240, 256), F32)])(
        zh.reshape(1), amps, other, mark
    )
    two = lax.all_to_all(two, ("x", "y", "core"), 0, 0, tiled=True)
    one = lax.all_to_all(one, "y", 0, 0, tiled=True)
    ordered = [w for pair in zip(along, across) for w in pair]
    partial = call(
        product_kernel, 0, 10, [(1152, 128)],
        [pltpu.VMEM((256, 768), BF16)] * 2 + [pltpu.VMEM((5, 192, 256), BF16)] * 2,
    )(one, two, *ordered)
    got = lax.all_to_all(partial.reshape(64, 1, 2304), ("y", "zh", "col"), 0, 0, tiled=True).reshape(1152, 128)
    r = ((x * 4 + y) * 2 + zh) * 2 + core
    place = jnp.stack([x, core, r * 3, col * 5, window_start[0]])
    new, inc = call(
        final_kernel, 3, 3, [(5, 3, 1152)] * 2,
        [pltpu.VMEM((192, 128), F32), pltpu.VMEM((3, 1152), F32), pltpu.VMEM((3, 1152), F32)],
    )(place, occupied_energy, virtual_energy, got, virtual_energy.reshape(1, 192), res)
    return jnp.transpose(new, (1, 0, 2)), jnp.transpose(inc, (1, 0, 2))


def solution(mesh):
    fine = Mesh(mesh.devices.reshape(SIZES), AXES)
    split = P(("x", "y", "zh", "core"), "col", None)
    return jax.shard_map(
        body, mesh=fine, in_specs=(split, split, split, P(), P(), P()), out_specs=(split, split), check_vma=False
    )
```

```python
import jax
import jax.numpy as jnp
from jax import lax
from jax.experimental import pallas as pl
from jax.experimental.pallas import tpu as pltpu
from jax.sharding import Mesh, PartitionSpec as P

AXES = ("x", "y", "zh", "core", "col")
SIZES = (4, 4, 2, 2, 8)
F32, BF16 = jnp.float32, jnp.bfloat16
VMEM = pl.BlockSpec(memory_space=pltpu.VMEM)
SMEM = pl.BlockSpec(memory_space=pltpu.SMEM)
NT = (((1,), (1,)), ((), ()))
NN = (((1,), (0,)), ((), ()))


def index(shape, axis):
    return lax.broadcasted_iota(jnp.int32, shape, axis)


def third(n, count):
    return sum((n >= 3 * s).astype(jnp.int32) for s in range(1, count))


def hot(mask):
    return jnp.where(mask, 1.0, 0.0).astype(BF16)


def order_matrix():
    n = index((1, 256), 1)
    q = n & 7
    zh = third(q, 2)
    v = ((n >> 4) & 3) * 48 + (n >> 6) * 12 + zh * 6 + ((n >> 3) & 1) * 3 + q - zh * 3
    v = jnp.where(q < 6, v, -1)
    return hot(index((256, 256), 0) == v)


def choose_matrix():
    n = index((1, 256), 1)
    block = sum((n >= 24 * s).astype(jnp.int32) for s in range(1, 11))
    q = n - block * 24
    yz = third(q, 8)
    v = (block >> 1) * 48 + (block & 1) * 3 + yz * 6 + q - yz * 3
    v = jnp.where(block < 8, v, -1)
    return hot(index((256, 256), 0) == v)


def turn_matrix():
    n = index((1, 768), 1)
    i, q = n >> 7, n & 127
    k = sum((q >= 24 * s).astype(jnp.int32) for s in range(1, 6))
    q = q - k * 24
    yz = third(q, 8)
    row = k * 192 + (yz >> 1) * 48 + (i & 1) * 24 + (yz & 1) * 9 + (i >> 1) * 3 + q - yz * 3
    row = jnp.where(k < 5, row, -1)
    return hot(index((960, 768), 0) == row)


def spread_matrix():
    n = index((1, 1280), 1)
    j, q = n >> 8, n & 255
    x = sum((q >= 48 * s).astype(jnp.int32) for s in range(1, 6))
    q = q - x * 48
    core = third(q, 2)
    row = (x * 2 + core) * 16 + j * 3 + q - core * 3
    row = jnp.where((x < 4) & (q < 6), row, -1)
    return hot(index((128, 1280), 0) == row)


def dot(a, b, dims=NN):
    return lax.dot_general(a, b, dims, preferred_element_type=F32)


def split2(v):
    high = v.astype(BF16)
    return high, (v - high.astype(F32)).astype(BF16)


def moved(v, hot):
    high = v.astype(BF16)
    rest = v - high.astype(F32)
    mid = rest.astype(BF16)
    low = (rest - mid.astype(F32)).astype(BF16)
    return (dot(low, hot) + dot(mid, hot)) + dot(high, hot)


def lanes192(ref, lead, n):
    if n % 2 == 0:
        return ref[lead, :, n * 192:n * 192 + 256]
    return pltpu.roll(ref[lead, :, n * 192 - 64:n * 192 + 192], 192, 1)


def weights_kernel(ints_ref, out_ref, mark_ref):
    out_ref[...] = jnp.zeros_like(out_ref)
    mark_ref[...] = jnp.zeros_like(mark_ref)
    lane = index((3, 128), 1)
    for k in range(5):
        for j in range(20):
            at = j // 5 * 16 + j % 5 * 3
            near = lanes192(ints_ref, k, j)
            far = pltpu.roll(lanes192(ints_ref, k, j + 20), 64, 1)
            out_ref[k, at:at + 3, :128] = near[:, :128]
            out_ref[k, at:at + 3, 128:256] = jnp.where(lane < 64, near[:, 128:], far[:, :128])
            out_ref[k, at:at + 3, 256:] = far[:, 128:]


def amps_kernel(zh_ref, own_ref, other_ref, mark_ref, one_ref, two_ref, rows):
    first = zh_ref[0] == 0
    rows[...] = jnp.zeros_like(rows)
    one_ref[...] = jnp.zeros_like(one_ref)
    for k in range(5):
        for p in range(3):
            own = own_ref[k, :, p * 384:(p + 1) * 384]
            other = other_ref[k, :, p * 384:(p + 1) * 384]
            for zh, v in ((0, jnp.where(first, own, other)), (1, jnp.where(first, other, own))):
                at = k * 24 + zh * 9 + p * 3
                one_ref[at:at + 3, :] = v
                at = k * 48 + p * 16 + zh * 3
                rows[at:at + 3, :] = v[:, :256]
                rows[at + 8:at + 11, :] = pltpu.roll(v[:, 128:], 192, 1)
    chosen = moved(rows[...], choose_matrix())
    lane = index((48, 128), 1)
    for n in range(8):
        part = jnp.zeros((48, 128), F32)
        for k in range(5):
            v = pltpu.roll(chosen[k * 48:(k + 1) * 48, :], (k * 24 - n * 24) % 256, 1)[:, :128]
            part = jnp.where((lane >= k * 24) & (lane < k * 24 + 24), v, part)
        two_ref[n] = part


def pack_kernel(one_ref, two_ref, out_ref):
    for y in range(4):
        for part in range(3):
            out_ref[y, part * 120:(part + 1) * 120, :] = one_ref[:, part * 128:(part + 1) * 128]
        out_ref[y, 360:, :] = two_ref[...].reshape(384, 128)


def combine_kernel(*refs):
    weights, high_ref, low_ref = refs[:8], refs[8], refs[9]
    for z in range(4):
        for k in range(5):
            rows = [ref[k, z * 16:(z + 1) * 16, :] for ref in weights]
            near = [v[:, :256] for v in rows]
            far = [pltpu.roll(v[:, 128:], 192, 1) for v in rows]
            high, low = split2(jnp.concatenate(near + far, 0))
            high_ref[z, k] = high
            low_ref[z, k] = low


def product_kernel(got_ref, high_ref, low_ref, out_ref, two_high, two_low, mixed_high, mixed_low):
    for i in range(6):
        starts = [360 + s * 48 + i * 8 for s in range(8)]
        part = jnp.concatenate([got_ref[y, at:at + 8, :] for y in range(4) for at in starts], 0)
        high, low = split2(part)
        two_high[:, i * 128:(i + 1) * 128] = high
        two_low[:, i * 128:(i + 1) * 128] = low
    order, turn = order_matrix(), turn_matrix()
    lane = index((24, 256), 1)
    for k in range(5):
        turn_k = turn[k * 192:(k + 1) * 192, :]
        swapped = dot(dot(turn_k, two_low[...], NT).astype(BF16), order, NT)
        swapped += dot(dot(turn_k, two_high[...], NT).astype(BF16), order, NT)
        straight = []
        for y in range(4):
            v = [got_ref[y, part * 120 + k * 24:part * 120 + (k + 1) * 24, :] for part in range(3)]
            near = jnp.concatenate(v[:2], 1)
            far = pltpu.roll(jnp.concatenate(v[1:], 1), 192, 1)
            straight.append(jnp.where(lane < 192, near, 0.0))
            straight.append(jnp.where(lane < 192, far, 0.0))
        high, low = split2(2.0 * jnp.concatenate(straight, 0) - swapped)
        mixed_high[k] = high
        mixed_low[k] = low
    for z in range(4):
        total = jnp.zeros((192, 256), F32)
        for k in range(5):
            high, low = high_ref[z, k], low_ref[z, k]
            total += dot(mixed_high[k], low, NT) + dot(mixed_low[k], high, NT) + dot(mixed_high[k], high, NT)
        for yz in range(8):
            for half in range(2):
                for e in range(2):
                    to = (yz * 8 + z + 4 * half) * 18 + e * 9
                    at = yz // 2 * 48 + e * 24 + yz % 2 * 9
                    out_ref[to:to + 9, :] = total[at:at + 9, half * 128:(half + 1) * 128]


def final_kernel(place_ref, occ_ref, va_ref, got_ref, vb_ref, res_ref, new_ref, inc_ref, sums, cyc, den):
    sums[...] = jnp.zeros_like(sums)
    for yz in range(8):
        total = got_ref[yz * 144:yz * 144 + 18, :]
        for z in range(1, 8):
            at = (yz * 8 + z) * 18
            total += got_ref[at:at + 18, :]
        sums[yz * 24:yz * 24 + 18, :] = total
    v = pltpu.roll(sums[...], place_ref[0] * 32, 1)
    lane = lax.broadcasted_iota(jnp.int32, v.shape, 1)
    other = jnp.where((lane & 16) == 0, pltpu.roll(v, 112, 1), pltpu.roll(v, 16, 1))
    v = jnp.where(place_ref[1] == 0, v, other)
    wide = moved(v, spread_matrix())
    row = lax.broadcasted_iota(jnp.int32, (3, 192), 0)
    va = [va_ref[place_ref[2] + m] for m in range(3)]
    va = jnp.where(row == 0, va[0], jnp.where(row == 1, va[1], va[2]))
    base = vb_ref[...] + va
    for i in range(6):
        den[:, i * 192:(i + 1) * 192] = base - occ_ref[place_ref[4] + i]
    for j in range(5):
        total = wide[0:24, j * 256:(j + 1) * 256]
        for yz in range(1, 8):
            total += pltpu.roll(wide[yz * 24:(yz + 1) * 24, j * 256:(j + 1) * 256], yz * 6, 1)
        for i in range(6):
            cyc[:, i * 192:(i + 1) * 192] = total[i % 2 * 9 + i // 2 * 3:i % 2 * 9 + i // 2 * 3 + 3, :192]
        new = res_ref[j] + cyc[...]
        new_ref[j] = new
        inc_ref[j] = new / (den[...] - occ_ref[place_ref[3] + j])


def call(kernel, n_smem, n_vmem, outs, scratch, mib=8, dtype=F32, cost=1):
    shapes = [jax.ShapeDtypeStruct(s, dtype) for s in outs]
    return pl.pallas_call(
        kernel,
        out_shape=shapes if len(shapes) > 1 else shapes[0],
        in_specs=[SMEM] * n_smem + [VMEM] * n_vmem,
        out_specs=[VMEM] * len(shapes) if len(shapes) > 1 else VMEM,
        scratch_shapes=scratch,
        cost_estimate=pl.CostEstimate(flops=cost * 10**9, bytes_accessed=1000, transcendentals=0),
        compiler_params=pltpu.CompilerParams(vmem_limit_bytes=mib * 1024 * 1024),
    )


def body(amplitudes, integrals, residual, occupied_energy, virtual_energy, window_start):
    x, y, zh, core, col = [lax.axis_index(a).astype(jnp.int32) for a in AXES]
    amps = jnp.transpose(amplitudes, (1, 0, 2))
    ints = jnp.transpose(integrals, (1, 0, 2))
    res = jnp.transpose(residual, (1, 0, 2))
    other = lax.ppermute(amps, "zh", [(0, 1), (1, 0)])
    weights, mark = call(weights_kernel, 0, 1, [(5, 64, 384), (8, 128)], [])(ints)
    along = [weights] + [
        lax.ppermute(weights, "x", [(s, (s - d) % 4) for s in range(4)]) for d in (1, 2, 3)
    ]
    across = [lax.ppermute(w, "core", [(0, 1), (1, 0)]) for w in along]
    one, two = call(amps_kernel, 1, 3, [(120, 384), (8, 48, 128)], [pltpu.VMEM((240, 256), F32)])(
        zh.reshape(1), amps, other, mark
    )
    two = lax.all_to_all(two, ("x", "core"), 0, 0, tiled=True)
    both = call(pack_kernel, 0, 2, [(4, 744, 128)], [])(one, two)
    both = lax.all_to_all(both, "y", 0, 0, tiled=True)
    ordered = [w for pair in zip(along, across) for w in pair]
    high, low = call(combine_kernel, 0, 8, [(4, 5, 256, 256)] * 2, [], 24, BF16, 5)(*ordered)
    partial = call(
        product_kernel, 0, 3, [(1152, 128)],
        [pltpu.VMEM((256, 768), BF16)] * 2 + [pltpu.VMEM((5, 192, 256), BF16)] * 2, 24,
    )(both, high, low)
    got = lax.all_to_all(partial.reshape(64, 1, 2304), ("y", "zh", "col"), 0, 0, tiled=True).reshape(1152, 128)
    r = ((x * 4 + y) * 2 + zh) * 2 + core
    place = jnp.stack([x, core, r * 3, col * 5, window_start[0]])
    new, inc = call(
        final_kernel, 3, 3, [(5, 3, 1152)] * 2,
        [pltpu.VMEM((192, 128), F32), pltpu.VMEM((3, 1152), F32), pltpu.VMEM((3, 1152), F32)],
    )(place, occupied_energy, virtual_energy, got, virtual_energy.reshape(1, 192), res)
    return jnp.transpose(new, (1, 0, 2)), jnp.transpose(inc, (1, 0, 2))


def solution(mesh):
    fine = Mesh(mesh.devices.reshape(SIZES), AXES)
    split = P(("x", "y", "zh", "core"), "col", None)
    return jax.shard_map(
        body, mesh=fine, in_specs=(split, split, split, P(), P(), P()), out_specs=(split, split), check_vma=False
    )
```

```python
import jax
import jax.numpy as jnp
from jax import lax
from jax.experimental import pallas as pl
from jax.experimental.pallas import tpu as pltpu
from jax.sharding import Mesh, PartitionSpec as P

AXES = ("x", "y", "zh", "core", "col")
SIZES = (4, 4, 2, 2, 8)
F32, BF16 = jnp.float32, jnp.bfloat16
VMEM = pl.BlockSpec(memory_space=pltpu.VMEM)
SMEM = pl.BlockSpec(memory_space=pltpu.SMEM)
NT = (((1,), (1,)), ((), ()))
NN = (((1,), (0,)), ((), ()))


def index(shape, axis):
    return lax.broadcasted_iota(jnp.int32, shape, axis)


def third(n, count):
    return sum((n >= 3 * s).astype(jnp.int32) for s in range(1, count))


def hot(mask):
    return jnp.where(mask, 1.0, 0.0).astype(BF16)


def order_matrix(e):
    n = index((1, 512), 1)
    v = ((n >> 5) & 3) * 48 + (n >> 7) * 12 + ((n >> 4) & 1) * 6 + ((n >> 3) & 1) * 3 + (n & 3)
    v = jnp.where(((n & 3) < 3) & (((n >> 2) & 1) == e), v, -1)
    return hot(index((256, 512), 0) == v)


def choose_matrix():
    n = index((1, 256), 1)
    block = sum((n >= 24 * s).astype(jnp.int32) for s in range(1, 11))
    q = n - block * 24
    yz = third(q, 8)
    v = (block >> 1) * 48 + (block & 1) * 3 + yz * 6 + q - yz * 3
    v = jnp.where(block < 8, v, -1)
    return hot(index((256, 256), 0) == v)


def turn_matrix():
    n = index((1, 384), 1)
    p, q = n >> 7, n & 127
    k = sum((q >= 24 * s).astype(jnp.int32) for s in range(1, 6))
    q = q - k * 24
    yz = third(q, 8)
    row = k * 96 + (yz >> 1) * 24 + (yz & 1) * 9 + p * 3 + q - yz * 3
    row = jnp.where(k < 5, row, -1)
    return hot(index((480, 384), 0) == row)


def spread_matrix():
    n = index((1, 1280), 1)
    j, q = n >> 8, n & 255
    x = sum((q >= 48 * s).astype(jnp.int32) for s in range(1, 6))
    q = q - x * 48
    core = third(q, 2)
    row = (x * 2 + core) * 16 + j * 3 + q - core * 3
    row = jnp.where((x < 4) & (q < 6), row, -1)
    return hot(index((128, 1280), 0) == row)


def dot(a, b, dims=NN):
    return lax.dot_general(a, b, dims, preferred_element_type=F32)


def split2(v):
    high = v.astype(BF16)
    return high, (v - high.astype(F32)).astype(BF16)


def moved(v, hot):
    high = v.astype(BF16)
    rest = v - high.astype(F32)
    mid = rest.astype(BF16)
    low = (rest - mid.astype(F32)).astype(BF16)
    return (dot(low, hot) + dot(mid, hot)) + dot(high, hot)


def lanes192(ref, lead, n):
    if n % 2 == 0:
        return ref[lead, :, n * 192:n * 192 + 256]
    return pltpu.roll(ref[lead, :, n * 192 - 64:n * 192 + 192], 192, 1)


def weights_kernel(ints_ref, out_ref):
    out_ref[...] = jnp.zeros_like(out_ref)
    lane = index((3, 128), 1)
    for k in range(5):
        for j in range(20):
            at = j // 5 * 16 + j % 5 * 3
            near = lanes192(ints_ref, k, j)
            far = pltpu.roll(lanes192(ints_ref, k, j + 20), 64, 1)
            out_ref[k, at:at + 3, :128] = near[:, :128]
            out_ref[k, at:at + 3, 128:256] = jnp.where(lane < 64, near[:, 128:], far[:, :128])
            out_ref[k, at:at + 3, 256:] = far[:, 128:]


def swap_kernel(own_ref, two_ref, rows):
    rows[...] = jnp.zeros_like(rows)
    for k in range(5):
        for p in range(3):
            v = own_ref[k, :, p * 384:(p + 1) * 384]
            at = k * 24 + p * 8
            rows[at:at + 3, :] = v[:, :256]
            rows[at + 4:at + 7, :] = pltpu.roll(v[:, 128:], 192, 1)
    chosen = moved(rows[...], choose_matrix())
    lane = index((24, 128), 1)
    for n in range(8):
        part = jnp.zeros((24, 128), F32)
        for k in range(5):
            v = pltpu.roll(chosen[k * 24:(k + 1) * 24, :], (k * 24 - n * 24) % 256, 1)[:, :128]
            part = jnp.where((lane >= k * 24) & (lane < k * 24 + 24), v, part)
        for zh in range(2):
            two_ref[n // 2 * 4 + zh * 2 + n % 2] = part


def pack_kernel(zh_ref, own_ref, other_ref, two_ref, out_ref, rows):
    first = zh_ref[0] == 0
    rows[...] = jnp.zeros_like(rows)
    for k in range(5):
        for p in range(3):
            own = own_ref[k, :, p * 384:(p + 1) * 384]
            other = other_ref[k, :, p * 384:(p + 1) * 384]
            at = k * 18 + p * 3
            rows[at:at + 3, :] = jnp.where(first, own, other)
            rows[at + 9:at + 12, :] = jnp.where(first, other, own)
    for y in range(4):
        for part in range(3):
            out_ref[y, part * 96:(part + 1) * 96, :] = rows[:, part * 128:(part + 1) * 128]
        out_ref[y, 288:, :] = two_ref[...].reshape(384, 128)


def mark_kernel(*refs):
    refs[-1][...] = jnp.zeros_like(refs[-1])


def product_kernel(got_ref, *refs):
    away, out_ref = refs[:8], refs[9]
    two_high, two_low, mixed_high, mixed_low, weights, arrived = refs[10:]
    copies = [pltpu.make_async_copy(away[n], weights.at[n], arrived.at[n]) for n in range(8)]
    for copy in copies:
        copy.start()
    for p in range(3):
        starts = [288 + s * 24 + p * 8 for s in range(16)]
        part = jnp.concatenate([got_ref[y, at:at + 8, :] for y in range(4) for at in starts], 0)
        high, low = split2(part)
        two_high[:, p * 128:(p + 1) * 128] = high
        two_low[:, p * 128:(p + 1) * 128] = low
    orders, turn = [order_matrix(0), order_matrix(1)], turn_matrix()
    lane = index((24, 256), 1)
    for k in range(5):
        turn_k = turn[k * 96:(k + 1) * 96, :]
        high = dot(turn_k, two_high[...], NT).astype(BF16)
        low = dot(turn_k, two_low[...], NT).astype(BF16)
        swapped = [dot(low, o, NT) + dot(high, o, NT) for o in orders]
        mixed = []
        for y in range(4):
            v = [got_ref[y, part * 96 + k * 18:part * 96 + k * 18 + 24, :] for part in range(3)]
            near = jnp.concatenate(v[:2], 1)
            far = pltpu.roll(jnp.concatenate(v[1:], 1), 192, 1)
            for e, straight in enumerate((near, far)):
                mixed.append(2.0 * jnp.where(lane < 192, straight, 0.0) - swapped[e][y * 24:(y + 1) * 24, :])
        high, low = split2(jnp.concatenate(mixed, 0))
        mixed_high[k] = high
        mixed_low[k] = low
    for copy in copies:
        copy.wait()
    for z in range(4):
        total = jnp.zeros((192, 256), F32)
        for k in range(5):
            rows = [weights[n, k, z * 16:(z + 1) * 16, :] for n in range(8)]
            near = [v[:, :256] for v in rows]
            far = [pltpu.roll(v[:, 128:], 192, 1) for v in rows]
            high, low = split2(jnp.concatenate(near + far, 0))
            total += dot(mixed_high[k], low, NT) + dot(mixed_low[k], high, NT) + dot(mixed_high[k], high, NT)
        for yz in range(8):
            for half in range(2):
                for e in range(2):
                    to = (yz * 8 + z + 4 * half) * 18 + e * 9
                    at = yz // 2 * 48 + e * 24 + yz % 2 * 9
                    out_ref[to:to + 9, :] = total[at:at + 9, half * 128:(half + 1) * 128]


def final_kernel(place_ref, occ_ref, va_ref, got_ref, vb_ref, res_ref, new_ref, inc_ref, sums, cyc, den):
    sums[...] = jnp.zeros_like(sums)
    for yz in range(8):
        total = got_ref[yz * 144:yz * 144 + 18, :]
        for z in range(1, 8):
            at = (yz * 8 + z) * 18
            total += got_ref[at:at + 18, :]
        sums[yz * 24:yz * 24 + 18, :] = total
    v = pltpu.roll(sums[...], place_ref[0] * 32, 1)
    lane = lax.broadcasted_iota(jnp.int32, v.shape, 1)
    other = jnp.where((lane & 16) == 0, pltpu.roll(v, 112, 1), pltpu.roll(v, 16, 1))
    v = jnp.where(place_ref[1] == 0, v, other)
    wide = moved(v, spread_matrix())
    row = lax.broadcasted_iota(jnp.int32, (3, 192), 0)
    va = [va_ref[place_ref[2] + m] for m in range(3)]
    va = jnp.where(row == 0, va[0], jnp.where(row == 1, va[1], va[2]))
    base = vb_ref[...] + va
    for i in range(6):
        den[:, i * 192:(i + 1) * 192] = base - occ_ref[place_ref[4] + i]
    for j in range(5):
        total = wide[0:24, j * 256:(j + 1) * 256]
        for yz in range(1, 8):
            total += pltpu.roll(wide[yz * 24:(yz + 1) * 24, j * 256:(j + 1) * 256], yz * 6, 1)
        for i in range(6):
            cyc[:, i * 192:(i + 1) * 192] = total[i % 2 * 9 + i // 2 * 3:i % 2 * 9 + i // 2 * 3 + 3, :192]
        new = res_ref[j] + cyc[...]
        new_ref[j] = new
        inc_ref[j] = new / (den[...] - occ_ref[place_ref[3] + j])


def call(kernel, n_smem, n_vmem, outs, scratch, mib=8, dtype=F32, cost=1, space=pltpu.VMEM):
    shapes = [jax.ShapeDtypeStruct(s, dtype) for s in outs]
    return pl.pallas_call(
        kernel,
        out_shape=shapes if len(shapes) > 1 else shapes[0],
        in_specs=[SMEM] * n_smem + [pl.BlockSpec(memory_space=space)] * n_vmem,
        out_specs=[VMEM] * len(shapes) if len(shapes) > 1 else VMEM,
        scratch_shapes=scratch,
        cost_estimate=pl.CostEstimate(flops=cost * 10**9, bytes_accessed=1000, transcendentals=0),
        compiler_params=pltpu.CompilerParams(vmem_limit_bytes=mib * 1024 * 1024),
    )


def body(amplitudes, integrals, residual, occupied_energy, virtual_energy, window_start):
    x, y, zh, core, col = [lax.axis_index(a).astype(jnp.int32) for a in AXES]
    amps = jnp.transpose(amplitudes, (1, 0, 2))
    ints = jnp.transpose(integrals, (1, 0, 2))
    res = jnp.transpose(residual, (1, 0, 2))
    other = lax.ppermute(amps, "zh", [(0, 1), (1, 0)])
    weights = call(weights_kernel, 0, 1, [(5, 64, 384)], [])(ints)
    along = [weights] + [
        lax.ppermute(weights, "x", [(s, (s - d) % 4) for s in range(4)]) for d in (1, 2, 3)
    ]
    across = [lax.ppermute(w, "core", [(0, 1), (1, 0)]) for w in along]
    two = call(swap_kernel, 0, 1, [(16, 24, 128)], [pltpu.VMEM((120, 256), F32)])(amps)
    two = lax.all_to_all(two, ("x", "zh", "core"), 0, 0, tiled=True)
    both = call(pack_kernel, 1, 3, [(4, 672, 128)], [pltpu.VMEM((96, 384), F32)])(zh.reshape(1), amps, other, two)
    both = lax.all_to_all(both, "y", 0, 0, tiled=True)
    ordered = [w for pair in zip(along, across) for w in pair]
    mark = call(mark_kernel, 0, 8, [(8, 128)], [], 8, F32, 1, pl.ANY)(*ordered)
    partial = pl.pallas_call(
        product_kernel,
        out_shape=jax.ShapeDtypeStruct((1152, 128), F32),
        in_specs=[VMEM] + [pl.BlockSpec(memory_space=pl.ANY)] * 9,
        out_specs=VMEM,
        scratch_shapes=[pltpu.VMEM((512, 384), BF16)] * 2 + [pltpu.VMEM((5, 192, 256), BF16)] * 2
        + [pltpu.VMEM((8, 5, 64, 384), F32), pltpu.SemaphoreType.DMA((8,))],
        cost_estimate=pl.CostEstimate(flops=10**9, bytes_accessed=1000, transcendentals=0),
        compiler_params=pltpu.CompilerParams(vmem_limit_bytes=52 * 1024 * 1024),
    )(both, *ordered, mark)
    got = lax.all_to_all(partial.reshape(64, 1, 2304), ("y", "zh", "col"), 0, 0, tiled=True).reshape(1152, 128)
    r = ((x * 4 + y) * 2 + zh) * 2 + core
    place = jnp.stack([x, core, r * 3, col * 5, window_start[0]])
    new, inc = call(
        final_kernel, 3, 3, [(5, 3, 1152)] * 2,
        [pltpu.VMEM((192, 128), F32), pltpu.VMEM((3, 1152), F32), pltpu.VMEM((3, 1152), F32)],
    )(place, occupied_energy, virtual_energy, got, virtual_energy.reshape(1, 192), res)
    return jnp.transpose(new, (1, 0, 2)), jnp.transpose(inc, (1, 0, 2))


def solution(mesh):
    fine = Mesh(mesh.devices.reshape(SIZES), AXES)
    split = P(("x", "y", "zh", "core"), "col", None)
    return jax.shard_map(
        body, mesh=fine, in_specs=(split, split, split, P(), P(), P()), out_specs=(split, split), check_vma=False
    )
```

```python
import jax
import jax.numpy as jnp
from jax import lax
from jax.experimental import pallas as pl
from jax.experimental.pallas import tpu as pltpu
from jax.sharding import Mesh, PartitionSpec as P

AXES = ("x", "y", "zh", "core", "pair", "par")
SIZES = (4, 4, 2, 2, 4, 2)
F32, BF16 = jnp.float32, jnp.bfloat16
VMEM = pl.BlockSpec(memory_space=pltpu.VMEM)
SMEM = pl.BlockSpec(memory_space=pltpu.SMEM)
NT = (((1,), (1,)), ((), ()))
NN = (((1,), (0,)), ((), ()))


def index(shape, axis):
    return lax.broadcasted_iota(jnp.int32, shape, axis)


def third(n, count):
    return sum((n >= 3 * s).astype(jnp.int32) for s in range(1, count))


def hot(mask):
    return jnp.where(mask, 1.0, 0.0).astype(BF16)


def order_matrix(e):
    n = index((1, 512), 1)
    v = ((n >> 5) & 3) * 48 + (n >> 7) * 12 + ((n >> 4) & 1) * 6 + ((n >> 3) & 1) * 3 + (n & 3)
    v = jnp.where(((n & 3) < 3) & (((n >> 2) & 1) == e), v, -1)
    return hot(index((256, 512), 0) == v)


def choose_matrix():
    n = index((1, 256), 1)
    block = sum((n >= 24 * s).astype(jnp.int32) for s in range(1, 11))
    q = n - block * 24
    yz = third(q, 8)
    v = (block >> 1) * 48 + (block & 1) * 3 + yz * 6 + q - yz * 3
    v = jnp.where(block < 8, v, -1)
    return hot(index((256, 256), 0) == v)


def turn_matrix():
    n = index((1, 384), 1)
    p, q = n >> 7, n & 127
    k = sum((q >= 24 * s).astype(jnp.int32) for s in range(1, 6))
    q = q - k * 24
    yz = third(q, 8)
    row = k * 96 + (yz >> 1) * 24 + (yz & 1) * 9 + p * 3 + q - yz * 3
    row = jnp.where(k < 5, row, -1)
    return hot(index((480, 384), 0) == row)


def spread_matrix(par):
    n = index((1, 1280), 1)
    j, q = n >> 8, n & 255
    slot = jnp.where((j & 1) == par, (j - par) >> 1, (j >> 1) + 3 - par)
    x = sum((q >= 48 * s).astype(jnp.int32) for s in range(1, 6))
    q = q - x * 48
    core = third(q, 2)
    row = (x * 2 + core) * 16 + slot * 3 + q - core * 3
    row = jnp.where((x < 4) & (q < 6), row, -1)
    return hot(index((128, 1280), 0) == row)


def dot(a, b, dims=NN):
    return lax.dot_general(a, b, dims, preferred_element_type=F32)


def split2(v):
    high = v.astype(BF16)
    return high, (v - high.astype(F32)).astype(BF16)


def moved(v, hot):
    high = v.astype(BF16)
    rest = v - high.astype(F32)
    mid = rest.astype(BF16)
    low = (rest - mid.astype(F32)).astype(BF16)
    return (dot(low, hot) + dot(mid, hot)) + dot(high, hot)


def weights_kernel(ints_ref, out_ref):
    out_ref[...] = jnp.zeros_like(out_ref)
    for k in range(5):
        for n in range(20):
            at = n // 5 * 16 + n % 5 * 3
            out_ref[k, at:at + 3, :] = ints_ref[k, :, n * 384:(n + 1) * 384]


def swap_kernel(own_ref, token_ref, two_ref, rows):
    rows[...] = jnp.zeros_like(rows)
    for k in range(5):
        for p in range(3):
            v = own_ref[k, :, p * 384:(p + 1) * 384]
            at = k * 24 + p * 8
            rows[at:at + 3, :] = v[:, :256]
            rows[at + 4:at + 7, :] = pltpu.roll(v[:, 128:], 192, 1)
    chosen = moved(rows[...], choose_matrix())
    lane = index((24, 128), 1)
    for n in range(8):
        part = jnp.zeros((24, 128), F32)
        for k in range(5):
            v = pltpu.roll(chosen[k * 24:(k + 1) * 24, :], (k * 24 - n * 24) % 256, 1)[:, :128]
            part = jnp.where((lane >= k * 24) & (lane < k * 24 + 24), v, part)
        for zh in range(2):
            two_ref[n // 2 * 4 + zh * 2 + n % 2] = part


def pack_kernel(zh_ref, own_ref, other_ref, two_ref, out_ref, rows):
    first = zh_ref[0] == 0
    rows[...] = jnp.zeros_like(rows)
    for k in range(5):
        for p in range(3):
            own = own_ref[k, :, p * 384:(p + 1) * 384]
            other = other_ref[k, :, p * 384:(p + 1) * 384]
            at = k * 18 + p * 3
            rows[at:at + 3, :] = jnp.where(first, own, other)
            rows[at + 9:at + 12, :] = jnp.where(first, other, own)
    for y in range(4):
        for part in range(3):
            out_ref[y, part * 96:(part + 1) * 96, :] = rows[:, part * 128:(part + 1) * 128]
        out_ref[y, 288:, :] = two_ref[...].reshape(384, 128)


def mark_kernel(*refs):
    refs[-1][...] = jnp.zeros_like(refs[-1])


def product_kernel(par_ref, got_ref, *refs):
    away, (keep_ref, send_ref) = refs[:8], refs[9:11]
    two_high, two_low, swapped, whole, mixed, weights, arrived = refs[11:]
    copies = [pltpu.make_async_copy(away[n], weights.at[n], arrived.at[n]) for n in range(8)]
    for copy in copies:
        copy.start()
    for p in range(3):
        starts = [288 + s * 24 + p * 8 for s in range(16)]
        part = jnp.concatenate([got_ref[y, at:at + 8, :] for y in range(4) for at in starts], 0)
        high, low = split2(part)
        two_high[:, p * 128:(p + 1) * 128] = high
        two_low[:, p * 128:(p + 1) * 128] = low
    turn = turn_matrix()
    parts = [dot(turn, two[...], NT).astype(BF16) for two in (two_high, two_low)]
    parts = jnp.concatenate(parts, 0)
    for e in range(2):
        moved_parts = dot(parts, order_matrix(e), NT)
        swapped[e] = moved_parts[:480] + moved_parts[480:]
    lane = index((24, 256), 1)
    for k in range(5):
        for y in range(4):
            v = [got_ref[y, part * 96 + k * 18:part * 96 + k * 18 + 24, :] for part in range(3)]
            near = jnp.concatenate(v[:2], 1)
            far = pltpu.roll(jnp.concatenate(v[1:], 1), 192, 1)
            for e, straight in enumerate((near, far)):
                at = (k * 4 + y) * 24
                value = 2.0 * jnp.where(lane < 192, straight, 0.0) - swapped[e, at:at + 24, :]
                whole[y * 48 + e * 24:y * 48 + e * 24 + 24, :] = value
        high, low = split2(whole[...])
        mixed[k, :192] = high
        mixed[k, 192:] = low
    for copy in copies:
        copy.wait()
    even = par_ref[0] == 0
    slot = index((192, 128), 1) & 15
    for q in range(4):
        total = jnp.zeros((192, 256), F32)
        for k in range(5):
            rows = [weights[n, k, q * 16:(q + 1) * 16, :] for n in range(8)]
            near = [v[:, :256] for v in rows]
            far = [pltpu.roll(v[:, 128:], 192, 1) for v in rows]
            high, low = split2(jnp.concatenate(near + far, 0))
            both = dot(mixed[k], high, NT)
            total += dot(mixed[k, :192], low, NT) + both[192:]
            total += both[:192]
        near, far = total[:, :128], total[:, 128:]
        first = jnp.where(slot < 9, near, pltpu.roll(far, 9, 1))
        second = jnp.where(slot < 6, pltpu.roll(near, 119, 1), far)
        for ref, v in ((keep_ref, jnp.where(even, first, second)), (send_ref, jnp.where(even, second, first))):
            for yz in range(8):
                for e in range(2):
                    to = (yz * 4 + q) * 18 + e * 9
                    at = yz // 2 * 48 + e * 24 + yz % 2 * 9
                    ref[to:to + 9, :] = v[at:at + 9, :]


def final_kernel(place_ref, occ_ref, va_ref, got_ref, vb_ref, res_ref, new_ref, inc_ref, sums, cyc, den):
    sums[...] = jnp.zeros_like(sums)
    for yz in range(8):
        total = got_ref[yz * 72:yz * 72 + 18, :]
        for z in range(1, 4):
            at = (yz * 4 + z) * 18
            total += got_ref[at:at + 18, :]
        sums[yz * 24:yz * 24 + 18, :] = total
    v = pltpu.roll(sums[...], place_ref[0] * 32, 1)
    lane = lax.broadcasted_iota(jnp.int32, v.shape, 1)
    other = jnp.where((lane & 16) == 0, pltpu.roll(v, 112, 1), pltpu.roll(v, 16, 1))
    v = jnp.where(place_ref[1] == 0, v, other)
    wide = moved(v, spread_matrix(place_ref[5]))
    row = lax.broadcasted_iota(jnp.int32, (3, 192), 0)
    va = [va_ref[place_ref[2] + m] for m in range(3)]
    va = jnp.where(row == 0, va[0], jnp.where(row == 1, va[1], va[2]))
    base = vb_ref[...] + va
    for i in range(6):
        den[:, i * 192:(i + 1) * 192] = base - occ_ref[place_ref[4] + i]
    for j in range(5):
        total = wide[0:24, j * 256:(j + 1) * 256]
        for yz in range(1, 8):
            total += pltpu.roll(wide[yz * 24:(yz + 1) * 24, j * 256:(j + 1) * 256], yz * 6, 1)
        for i in range(6):
            cyc[:, i * 192:(i + 1) * 192] = total[i % 2 * 9 + i // 2 * 3:i % 2 * 9 + i // 2 * 3 + 3, :192]
        new = res_ref[j] + cyc[...]
        new_ref[j] = new
        inc_ref[j] = new / (den[...] - occ_ref[place_ref[3] + j])


def call(kernel, n_smem, n_vmem, outs, scratch, mib=8, dtype=F32, cost=1, space=pltpu.VMEM):
    shapes = [jax.ShapeDtypeStruct(s, dtype) for s in outs]
    return pl.pallas_call(
        kernel,
        out_shape=shapes if len(shapes) > 1 else shapes[0],
        in_specs=[SMEM] * n_smem + [pl.BlockSpec(memory_space=space)] * n_vmem,
        out_specs=[VMEM] * len(shapes) if len(shapes) > 1 else VMEM,
        scratch_shapes=scratch,
        cost_estimate=pl.CostEstimate(flops=cost * 10**9, bytes_accessed=1000, transcendentals=0),
        compiler_params=pltpu.CompilerParams(vmem_limit_bytes=mib * 1024 * 1024),
    )


def body(amplitudes, integrals, residual, occupied_energy, virtual_energy, window_start):
    x, y, zh, core, pair, par = [lax.axis_index(a).astype(jnp.int32) for a in AXES]
    amps = jnp.transpose(amplitudes, (1, 0, 2))
    ints = jnp.transpose(integrals, (1, 0, 2))
    res = jnp.transpose(residual, (1, 0, 2))
    other = lax.ppermute(amps, "zh", [(0, 1), (1, 0)])
    weights = call(weights_kernel, 0, 1, [(5, 64, 384)], [])(ints)
    along = [weights] + [
        lax.ppermute(weights, "x", [(s, (s - d) % 4) for s in range(4)]) for d in (1, 2, 3)
    ]
    across = [lax.ppermute(w, "core", [(0, 1), (1, 0)]) for w in along]
    two = call(swap_kernel, 0, 2, [(16, 24, 128)], [pltpu.VMEM((120, 256), F32)])(amps, weights)
    two = lax.all_to_all(two, ("x", "zh", "core"), 0, 0, tiled=True)
    both = call(pack_kernel, 1, 3, [(4, 672, 128)], [pltpu.VMEM((96, 384), F32)])(zh.reshape(1), amps, other, two)
    both = lax.all_to_all(both, "y", 0, 0, tiled=True)
    ordered = [w for pair in zip(along, across) for w in pair]
    mark = call(mark_kernel, 0, 8, [(8, 128)], [], 8, F32, 1, pl.ANY)(*ordered)
    keep, send = pl.pallas_call(
        product_kernel,
        out_shape=[jax.ShapeDtypeStruct((576, 128), F32)] * 2,
        in_specs=[SMEM, VMEM] + [pl.BlockSpec(memory_space=pl.ANY)] * 9,
        out_specs=[VMEM] * 2,
        scratch_shapes=[pltpu.VMEM((512, 384), BF16)] * 2
        + [pltpu.VMEM((2, 480, 256), F32), pltpu.VMEM((192, 256), F32), pltpu.VMEM((5, 384, 256), BF16)]
        + [pltpu.VMEM((8, 5, 64, 384), F32), pltpu.SemaphoreType.DMA((8,))],
        cost_estimate=pl.CostEstimate(flops=10**9, bytes_accessed=1000, transcendentals=0),
        compiler_params=pltpu.CompilerParams(vmem_limit_bytes=52 * 1024 * 1024),
    )(par.reshape(1), both, *ordered, mark)
    half = keep + lax.ppermute(send, "par", [(0, 1), (1, 0)])
    got = lax.all_to_all(half.reshape(32, 1, 2304), ("y", "zh", "pair"), 0, 0, tiled=True).reshape(576, 128)
    r = ((x * 4 + y) * 2 + zh) * 2 + core
    place = jnp.stack([x, core, r * 3, (pair * 2 + par) * 5, window_start[0], par])
    new, inc = call(
        final_kernel, 3, 3, [(5, 3, 1152)] * 2,
        [pltpu.VMEM((192, 128), F32), pltpu.VMEM((3, 1152), F32), pltpu.VMEM((3, 1152), F32)],
    )(place, occupied_energy, virtual_energy, got, virtual_energy.reshape(1, 192), res)
    return jnp.transpose(new, (1, 0, 2)), jnp.transpose(inc, (1, 0, 2))


def solution(mesh):
    fine = Mesh(mesh.devices.reshape(SIZES), AXES)
    split = P(("x", "y", "zh", "core"), ("pair", "par"), None)
    return jax.shard_map(
        body, mesh=fine, in_specs=(split, split, split, P(), P(), P()), out_specs=(split, split), check_vma=False
    )
```

```python
import jax
import jax.numpy as jnp
from jax import lax
from jax.experimental import pallas as pl
from jax.experimental.pallas import tpu as pltpu
from jax.sharding import Mesh, PartitionSpec as P

AXES = ("x", "y", "zh", "core", "pair", "par")
SIZES = (4, 4, 2, 2, 4, 2)
F32, BF16 = jnp.float32, jnp.bfloat16
VMEM = pl.BlockSpec(memory_space=pltpu.VMEM)
SMEM = pl.BlockSpec(memory_space=pltpu.SMEM)
NT = (((1,), (1,)), ((), ()))
NN = (((1,), (0,)), ((), ()))


def index(shape, axis):
    return lax.broadcasted_iota(jnp.int32, shape, axis)


def third(n, count):
    return sum((n >= 3 * s).astype(jnp.int32) for s in range(1, count))


def hot(mask):
    return jnp.where(mask, 1.0, 0.0).astype(BF16)


def order_matrix(e):
    n = index((1, 512), 1)
    v = ((n >> 5) & 3) * 48 + (n >> 7) * 12 + ((n >> 4) & 1) * 6 + ((n >> 3) & 1) * 3 + (n & 3)
    v = jnp.where(((n & 3) < 3) & (((n >> 2) & 1) == e), v, -1)
    return hot(index((256, 512), 0) == v)


def choose_matrix():
    n = index((1, 256), 1)
    block = sum((n >= 24 * s).astype(jnp.int32) for s in range(1, 11))
    q = n - block * 24
    yz = third(q, 8)
    v = (block >> 1) * 48 + (block & 1) * 3 + yz * 6 + q - yz * 3
    v = jnp.where(block < 8, v, -1)
    return hot(index((256, 256), 0) == v)


def turn_matrix():
    n = index((1, 384), 1)
    p, q = n >> 7, n & 127
    k = sum((q >= 24 * s).astype(jnp.int32) for s in range(1, 6))
    q = q - k * 24
    yz = third(q, 8)
    row = k * 96 + (yz >> 1) * 24 + (yz & 1) * 9 + p * 3 + q - yz * 3
    row = jnp.where(k < 5, row, -1)
    return hot(index((480, 384), 0) == row)


def spread_matrix(par):
    n = index((1, 1280), 1)
    j, q = n >> 8, n & 255
    slot = jnp.where((j & 1) == par, (j - par) >> 1, (j >> 1) + 3 - par)
    x = sum((q >= 48 * s).astype(jnp.int32) for s in range(1, 6))
    q = q - x * 48
    core = third(q, 2)
    row = (x * 2 + core) * 16 + slot * 3 + q - core * 3
    row = jnp.where((x < 4) & (q < 6), row, -1)
    return hot(index((128, 1280), 0) == row)


def dot(a, b, dims=NN):
    return lax.dot_general(a, b, dims, preferred_element_type=F32)


def split2(v):
    high = v.astype(BF16)
    return high, (v - high.astype(F32)).astype(BF16)


def moved(v, hot):
    high = v.astype(BF16)
    rest = v - high.astype(F32)
    mid = rest.astype(BF16)
    low = (rest - mid.astype(F32)).astype(BF16)
    return (dot(low, hot) + dot(mid, hot)) + dot(high, hot)


def weights_kernel(ints_ref, token_ref, out_ref):
    out_ref[...] = jnp.zeros_like(out_ref)
    for k in range(5):
        for n in range(20):
            at = n // 5 * 16 + n % 5 * 3
            out_ref[k, at:at + 3, :] = ints_ref[k, :, n * 384:(n + 1) * 384]


def swap_kernel(own_ref, two_ref, rows):
    rows[...] = jnp.zeros_like(rows)
    for k in range(5):
        for p in range(3):
            v = own_ref[k, :, p * 384:(p + 1) * 384]
            at = k * 24 + p * 8
            rows[at:at + 3, :] = v[:, :256]
            rows[at + 4:at + 7, :] = pltpu.roll(v[:, 128:], 192, 1)
    chosen = moved(rows[...], choose_matrix())
    lane = index((24, 128), 1)
    for n in range(8):
        part = jnp.zeros((24, 128), F32)
        for k in range(5):
            v = pltpu.roll(chosen[k * 24:(k + 1) * 24, :], (k * 24 - n * 24) % 256, 1)[:, :128]
            part = jnp.where((lane >= k * 24) & (lane < k * 24 + 24), v, part)
        for zh in range(2):
            two_ref[n // 2 * 4 + zh * 2 + n % 2] = part


def merge_kernel(zh_ref, own_ref, other_ref, out_ref, rows):
    first = zh_ref[0] == 0
    rows[...] = jnp.zeros_like(rows)
    for k in range(5):
        for p in range(3):
            own = own_ref[k, :, p * 384:(p + 1) * 384]
            other = other_ref[k, :, p * 384:(p + 1) * 384]
            at = k * 18 + p * 3
            rows[at:at + 3, :] = jnp.where(first, own, other)
            rows[at + 9:at + 12, :] = jnp.where(first, other, own)
    for part in range(3):
        out_ref[part * 96:(part + 1) * 96, :] = rows[:, part * 128:(part + 1) * 128]


def pack_kernel(one_ref, two_ref, out_ref):
    for y in range(4):
        out_ref[y, :288, :] = one_ref[...]
        out_ref[y, 288:, :] = two_ref[...].reshape(384, 128)


def mark_kernel(*refs):
    refs[-1][...] = jnp.zeros_like(refs[-1])


def product_kernel(par_ref, got_ref, *refs):
    away, (keep_ref, send_ref) = refs[:8], refs[9:11]
    two_high, two_low, swapped, whole, mixed, weights, arrived = refs[11:]
    copies = [pltpu.make_async_copy(away[n], weights.at[n], arrived.at[n]) for n in range(8)]
    for copy in copies:
        copy.start()
    for p in range(3):
        starts = [288 + s * 24 + p * 8 for s in range(16)]
        part = jnp.concatenate([got_ref[y, at:at + 8, :] for y in range(4) for at in starts], 0)
        high, low = split2(part)
        two_high[:, p * 128:(p + 1) * 128] = high
        two_low[:, p * 128:(p + 1) * 128] = low
    turn = turn_matrix()
    parts = [dot(turn, two[...], NT).astype(BF16) for two in (two_high, two_low)]
    parts = jnp.concatenate(parts, 0)
    for e in range(2):
        moved_parts = dot(parts, order_matrix(e), NT)
        swapped[e] = moved_parts[:480] + moved_parts[480:]
    lane = index((24, 256), 1)
    for k in range(5):
        for y in range(4):
            v = [got_ref[y, part * 96 + k * 18:part * 96 + k * 18 + 24, :] for part in range(3)]
            near = jnp.concatenate(v[:2], 1)
            far = pltpu.roll(jnp.concatenate(v[1:], 1), 192, 1)
            for e, straight in enumerate((near, far)):
                at = (k * 4 + y) * 24
                value = 2.0 * jnp.where(lane < 192, straight, 0.0) - swapped[e, at:at + 24, :]
                whole[y * 48 + e * 24:y * 48 + e * 24 + 24, :] = value
        high, low = split2(whole[...])
        mixed[k, :192] = high
        mixed[k, 192:] = low
    for copy in copies:
        copy.wait()
    even = par_ref[0] == 0
    slot = index((192, 128), 1) & 15
    for q in range(4):
        total = jnp.zeros((192, 256), F32)
        for k in range(5):
            rows = [weights[n, k, q * 16:(q + 1) * 16, :] for n in range(8)]
            near = [v[:, :256] for v in rows]
            far = [pltpu.roll(v[:, 128:], 192, 1) for v in rows]
            high, low = split2(jnp.concatenate(near + far, 0))
            both = dot(mixed[k], high, NT)
            total += dot(mixed[k, :192], low, NT) + both[192:]
            total += both[:192]
        near, far = total[:, :128], total[:, 128:]
        first = jnp.where(slot < 9, near, pltpu.roll(far, 9, 1))
        second = jnp.where(slot < 6, pltpu.roll(near, 119, 1), far)
        for ref, v in ((keep_ref, jnp.where(even, first, second)), (send_ref, jnp.where(even, second, first))):
            for yz in range(8):
                for e in range(2):
                    to = (yz * 4 + q) * 18 + e * 9
                    at = yz // 2 * 48 + e * 24 + yz % 2 * 9
                    ref[to:to + 9, :] = v[at:at + 9, :]


def final_kernel(place_ref, occ_ref, va_ref, got_ref, vb_ref, res_ref, new_ref, inc_ref, sums, cyc, den):
    sums[...] = jnp.zeros_like(sums)
    for yz in range(8):
        total = got_ref[yz * 72:yz * 72 + 18, :]
        for z in range(1, 4):
            at = (yz * 4 + z) * 18
            total += got_ref[at:at + 18, :]
        sums[yz * 24:yz * 24 + 18, :] = total
    v = pltpu.roll(sums[...], place_ref[0] * 32, 1)
    lane = lax.broadcasted_iota(jnp.int32, v.shape, 1)
    other = jnp.where((lane & 16) == 0, pltpu.roll(v, 112, 1), pltpu.roll(v, 16, 1))
    v = jnp.where(place_ref[1] == 0, v, other)
    wide = moved(v, spread_matrix(place_ref[5]))
    row = lax.broadcasted_iota(jnp.int32, (3, 192), 0)
    va = [va_ref[place_ref[2] + m] for m in range(3)]
    va = jnp.where(row == 0, va[0], jnp.where(row == 1, va[1], va[2]))
    base = vb_ref[...] + va
    for i in range(6):
        den[:, i * 192:(i + 1) * 192] = base - occ_ref[place_ref[4] + i]
    for j in range(5):
        total = wide[0:24, j * 256:(j + 1) * 256]
        for yz in range(1, 8):
            total += pltpu.roll(wide[yz * 24:(yz + 1) * 24, j * 256:(j + 1) * 256], yz * 6, 1)
        for i in range(6):
            cyc[:, i * 192:(i + 1) * 192] = total[i % 2 * 9 + i // 2 * 3:i % 2 * 9 + i // 2 * 3 + 3, :192]
        new = res_ref[j] + cyc[...]
        new_ref[j] = new
        inc_ref[j] = new / (den[...] - occ_ref[place_ref[3] + j])


def call(kernel, n_smem, n_vmem, outs, scratch, mib=8, dtype=F32, cost=1, space=pltpu.VMEM):
    shapes = [jax.ShapeDtypeStruct(s, dtype) for s in outs]
    return pl.pallas_call(
        kernel,
        out_shape=shapes if len(shapes) > 1 else shapes[0],
        in_specs=[SMEM] * n_smem + [pl.BlockSpec(memory_space=space)] * n_vmem,
        out_specs=[VMEM] * len(shapes) if len(shapes) > 1 else VMEM,
        scratch_shapes=scratch,
        cost_estimate=pl.CostEstimate(flops=cost * 10**9, bytes_accessed=1000, transcendentals=0),
        compiler_params=pltpu.CompilerParams(vmem_limit_bytes=mib * 1024 * 1024),
    )


def body(amplitudes, integrals, residual, occupied_energy, virtual_energy, window_start):
    x, y, zh, core, pair, par = [lax.axis_index(a).astype(jnp.int32) for a in AXES]
    amps = jnp.transpose(amplitudes, (1, 0, 2))
    ints = jnp.transpose(integrals, (1, 0, 2))
    res = jnp.transpose(residual, (1, 0, 2))
    other = lax.ppermute(amps, "zh", [(0, 1), (1, 0)])
    two = call(swap_kernel, 0, 1, [(16, 24, 128)], [pltpu.VMEM((120, 256), F32)])(amps)
    weights = call(weights_kernel, 0, 2, [(5, 64, 384)], [])(ints, two)
    along = [weights] + [
        lax.ppermute(weights, "x", [(s, (s - d) % 4) for s in range(4)]) for d in (1, 2, 3)
    ]
    across = [lax.ppermute(w, "core", [(0, 1), (1, 0)]) for w in along]
    two = lax.all_to_all(two, ("x", "zh", "core"), 0, 0, tiled=True)
    one = call(merge_kernel, 1, 2, [(288, 128)], [pltpu.VMEM((96, 384), F32)], cost=8)(zh.reshape(1), amps, other)
    both = call(pack_kernel, 0, 2, [(4, 672, 128)], [])(one, two)
    both = lax.all_to_all(both, "y", 0, 0, tiled=True)
    ordered = [w for pair in zip(along, across) for w in pair]
    mark = call(mark_kernel, 0, 8, [(8, 128)], [], 8, F32, 1, pl.ANY)(*ordered)
    keep, send = pl.pallas_call(
        product_kernel,
        out_shape=[jax.ShapeDtypeStruct((576, 128), F32)] * 2,
        in_specs=[SMEM, VMEM] + [pl.BlockSpec(memory_space=pl.ANY)] * 9,
        out_specs=[VMEM] * 2,
        scratch_shapes=[pltpu.VMEM((512, 384), BF16)] * 2
        + [pltpu.VMEM((2, 480, 256), F32), pltpu.VMEM((192, 256), F32), pltpu.VMEM((5, 384, 256), BF16)]
        + [pltpu.VMEM((8, 5, 64, 384), F32), pltpu.SemaphoreType.DMA((8,))],
        cost_estimate=pl.CostEstimate(flops=10**9, bytes_accessed=1000, transcendentals=0),
        compiler_params=pltpu.CompilerParams(vmem_limit_bytes=52 * 1024 * 1024),
    )(par.reshape(1), both, *ordered, mark)
    half = keep + lax.ppermute(send, "par", [(0, 1), (1, 0)])
    got = lax.all_to_all(half.reshape(32, 1, 2304), ("y", "zh", "pair"), 0, 0, tiled=True).reshape(576, 128)
    r = ((x * 4 + y) * 2 + zh) * 2 + core
    place = jnp.stack([x, core, r * 3, (pair * 2 + par) * 5, window_start[0], par])
    new, inc = call(
        final_kernel, 3, 3, [(5, 3, 1152)] * 2,
        [pltpu.VMEM((192, 128), F32), pltpu.VMEM((3, 1152), F32), pltpu.VMEM((3, 1152), F32)],
    )(place, occupied_energy, virtual_energy, got, virtual_energy.reshape(1, 192), res)
    return jnp.transpose(new, (1, 0, 2)), jnp.transpose(inc, (1, 0, 2))


def solution(mesh):
    fine = Mesh(mesh.devices.reshape(SIZES), AXES)
    split = P(("x", "y", "zh", "core"), ("pair", "par"), None)
    return jax.shard_map(
        body, mesh=fine, in_specs=(split, split, split, P(), P(), P()), out_specs=(split, split), check_vma=False
    )
```

```python
import jax
import jax.numpy as jnp
from jax import lax
from jax.experimental import pallas as pl
from jax.experimental.pallas import tpu as pltpu
from jax.sharding import Mesh, PartitionSpec as P

AXES = ("x", "y", "zh", "core", "pair", "par")
SIZES = (4, 4, 2, 2, 4, 2)
F32, BF16 = jnp.float32, jnp.bfloat16
VMEM = pl.BlockSpec(memory_space=pltpu.VMEM)
SMEM = pl.BlockSpec(memory_space=pltpu.SMEM)
NT = (((1,), (1,)), ((), ()))
NN = (((1,), (0,)), ((), ()))


def index(shape, axis):
    return lax.broadcasted_iota(jnp.int32, shape, axis)


def third(n, count):
    return sum((n >= 3 * s).astype(jnp.int32) for s in range(1, count))


def hot(mask):
    return jnp.where(mask, 1.0, 0.0).astype(BF16)


def order_matrix(e):
    n = index((1, 384), 1)
    source = (n * 10923) >> 16
    m = n - source * 6 - e * 3
    v = ((source >> 2) & 3) * 48 + (source >> 4) * 12 + ((source >> 1) & 1) * 6 + (source & 1) * 3 + m
    v = jnp.where((m >= 0) & (m < 3), v, -1)
    return hot(index((256, 384), 0) == v)


def choose_matrix():
    n = index((1, 256), 1)
    block = sum((n >= 24 * s).astype(jnp.int32) for s in range(1, 11))
    q = n - block * 24
    yz = third(q, 8)
    v = (block >> 1) * 48 + (block & 1) * 3 + yz * 6 + q - yz * 3
    v = jnp.where(block < 8, v, -1)
    return hot(index((256, 256), 0) == v)


def turn_matrix():
    n = index((1, 384), 1)
    p, q = n >> 7, n & 127
    k = sum((q >= 24 * s).astype(jnp.int32) for s in range(1, 6))
    q = q - k * 24
    yz = third(q, 8)
    row = k * 96 + (yz >> 1) * 24 + (yz & 1) * 9 + p * 3 + q - yz * 3
    row = jnp.where(k < 5, row, -1)
    return hot(index((480, 384), 0) == row)


def spread_matrix(par):
    n = index((1, 1280), 1)
    j, q = n >> 8, n & 255
    slot = jnp.where((j & 1) == par, (j - par) >> 1, (j >> 1) + 3 - par)
    x = sum((q >= 48 * s).astype(jnp.int32) for s in range(1, 6))
    q = q - x * 48
    core = third(q, 2)
    row = (x * 2 + core) * 16 + slot * 3 + q - core * 3
    row = jnp.where((x < 4) & (q < 6), row, -1)
    return hot(index((128, 1280), 0) == row)


def dot(a, b, dims=NN):
    return lax.dot_general(a, b, dims, preferred_element_type=F32)


def split2(v):
    high = v.astype(BF16)
    return high, (v - high.astype(F32)).astype(BF16)


def moved(v, hot):
    high = v.astype(BF16)
    rest = v - high.astype(F32)
    mid = rest.astype(BF16)
    low = (rest - mid.astype(F32)).astype(BF16)
    return (dot(low, hot) + dot(mid, hot)) + dot(high, hot)


def weights_kernel(ints_ref, token_ref, out_ref):
    out_ref[...] = jnp.zeros_like(out_ref)
    for k in range(5):
        for n in range(20):
            at = n // 5 * 16 + n % 5 * 3
            out_ref[k, at:at + 3, :] = ints_ref[k, :, n * 384:(n + 1) * 384]


def swap_kernel(own_ref, two_ref, rows):
    rows[...] = jnp.zeros_like(rows)
    for k in range(5):
        for p in range(3):
            v = own_ref[k, :, p * 384:(p + 1) * 384]
            at = k * 24 + p * 6
            rows[at:at + 3, :] = v[:, :256]
            rows[at + 3:at + 6, :] = pltpu.roll(v[:, 128:], 192, 1)
    chosen = moved(rows[...], choose_matrix())
    lane = index((24, 128), 1)
    for n in range(8):
        part = jnp.zeros((24, 128), F32)
        for k in range(5):
            v = pltpu.roll(chosen[k * 24:(k + 1) * 24, :], (k * 24 - n * 24) % 256, 1)[:, :128]
            part = jnp.where((lane >= k * 24) & (lane < k * 24 + 24), v, part)
        for zh in range(2):
            two_ref[n // 2 * 4 + zh * 2 + n % 2] = part


def merge_kernel(zh_ref, own_ref, other_ref, out_ref, rows):
    first = zh_ref[0] == 0
    rows[...] = jnp.zeros_like(rows)
    for k in range(5):
        for p in range(3):
            own = own_ref[k, :, p * 384:(p + 1) * 384]
            other = other_ref[k, :, p * 384:(p + 1) * 384]
            at = k * 18 + p * 3
            rows[at:at + 3, :] = jnp.where(first, own, other)
            rows[at + 9:at + 12, :] = jnp.where(first, other, own)
    for part in range(3):
        out_ref[part * 96:(part + 1) * 96, :] = rows[:, part * 128:(part + 1) * 128]


def pack_kernel(one_ref, two_ref, out_ref):
    for y in range(4):
        out_ref[y, :288, :] = one_ref[...]
        for n in range(16):
            out_ref[y, 288 + n * 18:306 + n * 18, :] = two_ref[n, :18, :]


def mark_kernel(*refs):
    refs[-1][...] = jnp.zeros_like(refs[-1])


def product_kernel(par_ref, got_ref, *refs):
    away, (keep_ref, send_ref) = refs[:8], refs[9:11]
    two_high, two_low, stage, swapped, whole, mixed, weights, arrived = refs[11:]
    copies = [pltpu.make_async_copy(away[n], weights.at[n], arrived.at[n]) for n in range(8)]
    for copy in copies:
        copy.start()
    for p in range(3):
        for y in range(4):
            for n in range(16):
                at = 288 + n * 18 + p * 6
                stage[y * 96 + n * 6:y * 96 + n * 6 + 6, :] = got_ref[y, at:at + 6, :]
        high, low = split2(stage[...])
        two_high[:, p * 128:(p + 1) * 128] = high
        two_low[:, p * 128:(p + 1) * 128] = low
    turn = turn_matrix()
    parts = [dot(turn, two[...], NT).astype(BF16) for two in (two_high, two_low)]
    parts = jnp.concatenate(parts, 0)
    for e in range(2):
        moved_parts = dot(parts, order_matrix(e), NT)
        swapped[e] = moved_parts[:480] + moved_parts[480:]
    lane = index((24, 256), 1)
    for k in range(5):
        for y in range(4):
            v = [got_ref[y, part * 96 + k * 18:part * 96 + k * 18 + 24, :] for part in range(3)]
            near = jnp.concatenate(v[:2], 1)
            far = pltpu.roll(jnp.concatenate(v[1:], 1), 192, 1)
            for e, straight in enumerate((near, far)):
                at = (k * 4 + y) * 24
                value = 2.0 * jnp.where(lane < 192, straight, 0.0) - swapped[e, at:at + 24, :]
                whole[y * 48 + e * 24:y * 48 + e * 24 + 24, :] = value
        high, low = split2(whole[...])
        mixed[k, :192] = high
        mixed[k, 192:] = low
    for copy in copies:
        copy.wait()
    even = par_ref[0] == 0
    slot = index((192, 128), 1) & 15
    for q in range(4):
        total = jnp.zeros((192, 256), F32)
        for k in range(5):
            rows = [weights[n, k, q * 16:(q + 1) * 16, :] for n in range(8)]
            near = [v[:, :256] for v in rows]
            far = [pltpu.roll(v[:, 128:], 192, 1) for v in rows]
            high, low = split2(jnp.concatenate(near + far, 0))
            both = dot(mixed[k], high, NT)
            total += dot(mixed[k, :192], low, NT) + both[192:]
            total += both[:192]
        near, far = total[:, :128], total[:, 128:]
        first = jnp.where(slot < 9, near, pltpu.roll(far, 9, 1))
        second = jnp.where(slot < 6, pltpu.roll(near, 119, 1), far)
        for ref, v in ((keep_ref, jnp.where(even, first, second)), (send_ref, jnp.where(even, second, first))):
            for yz in range(8):
                for e in range(2):
                    to = (yz * 4 + q) * 18 + e * 9
                    at = yz // 2 * 48 + e * 24 + yz % 2 * 9
                    ref[to:to + 9, :] = v[at:at + 9, :]


def final_kernel(place_ref, occ_ref, va_ref, got_ref, vb_ref, res_ref, new_ref, inc_ref, sums, cyc, den):
    sums[...] = jnp.zeros_like(sums)
    for yz in range(8):
        total = got_ref[yz * 72:yz * 72 + 18, :]
        for z in range(1, 4):
            at = (yz * 4 + z) * 18
            total += got_ref[at:at + 18, :]
        sums[yz * 24:yz * 24 + 18, :] = total
    v = pltpu.roll(sums[...], place_ref[0] * 32, 1)
    lane = lax.broadcasted_iota(jnp.int32, v.shape, 1)
    other = jnp.where((lane & 16) == 0, pltpu.roll(v, 112, 1), pltpu.roll(v, 16, 1))
    v = jnp.where(place_ref[1] == 0, v, other)
    wide = moved(v, spread_matrix(place_ref[5]))
    row = lax.broadcasted_iota(jnp.int32, (3, 192), 0)
    va = [va_ref[place_ref[2] + m] for m in range(3)]
    va = jnp.where(row == 0, va[0], jnp.where(row == 1, va[1], va[2]))
    base = vb_ref[...] + va
    for i in range(6):
        den[:, i * 192:(i + 1) * 192] = base - occ_ref[place_ref[4] + i]
    for j in range(5):
        total = wide[0:24, j * 256:(j + 1) * 256]
        for yz in range(1, 8):
            total += pltpu.roll(wide[yz * 24:(yz + 1) * 24, j * 256:(j + 1) * 256], yz * 6, 1)
        for i in range(6):
            cyc[:, i * 192:(i + 1) * 192] = total[i % 2 * 9 + i // 2 * 3:i % 2 * 9 + i // 2 * 3 + 3, :192]
        new = res_ref[j] + cyc[...]
        new_ref[j] = new
        inc_ref[j] = new / (den[...] - occ_ref[place_ref[3] + j])


def call(kernel, n_smem, n_vmem, outs, scratch, mib=8, dtype=F32, cost=1000, space=pltpu.VMEM):
    shapes = [jax.ShapeDtypeStruct(s, dtype) for s in outs]
    return pl.pallas_call(
        kernel,
        out_shape=shapes if len(shapes) > 1 else shapes[0],
        in_specs=[SMEM] * n_smem + [pl.BlockSpec(memory_space=space)] * n_vmem,
        out_specs=[VMEM] * len(shapes) if len(shapes) > 1 else VMEM,
        scratch_shapes=scratch,
        cost_estimate=pl.CostEstimate(flops=cost * 10**6, bytes_accessed=1000, transcendentals=0),
        compiler_params=pltpu.CompilerParams(vmem_limit_bytes=mib * 1024 * 1024),
    )


def body(amplitudes, integrals, residual, occupied_energy, virtual_energy, window_start):
    x, y, zh, core, pair, par = [lax.axis_index(a).astype(jnp.int32) for a in AXES]
    amps = jnp.transpose(amplitudes, (1, 0, 2))
    ints = jnp.transpose(integrals, (1, 0, 2))
    res = jnp.transpose(residual, (1, 0, 2))
    other = lax.ppermute(amps, "zh", [(0, 1), (1, 0)])
    two = call(swap_kernel, 0, 1, [(16, 24, 128)], [pltpu.VMEM((120, 256), F32)])(amps)
    weights = call(weights_kernel, 0, 2, [(5, 64, 384)], [])(ints, two)
    along = [weights] + [
        lax.ppermute(weights, "x", [(s, (s - d) % 4) for s in range(4)]) for d in (1, 3, 2)
    ]
    across = [lax.ppermute(w, "core", [(0, 1), (1, 0)]) for w in along]
    two = lax.all_to_all(two, ("x", "zh", "core"), 0, 0, tiled=True)
    one = call(merge_kernel, 1, 2, [(288, 128)], [pltpu.VMEM((96, 384), F32)], cost=8000)(zh.reshape(1), amps, other)
    both = call(pack_kernel, 0, 2, [(4, 576, 128)], [])(one, two)
    both = lax.all_to_all(both, "y", 0, 0, tiled=True)
    ordered = [w for pair in zip(along, across) for w in pair]
    ordered = ordered[:4] + ordered[6:] + ordered[4:6]
    mark = call(mark_kernel, 0, 8, [(8, 128)], [], 8, F32, 1000, pl.ANY)(*ordered)
    keep, send = pl.pallas_call(
        product_kernel,
        out_shape=[jax.ShapeDtypeStruct((576, 128), F32)] * 2,
        in_specs=[SMEM, VMEM] + [pl.BlockSpec(memory_space=pl.ANY)] * 9,
        out_specs=[VMEM] * 2,
        scratch_shapes=[pltpu.VMEM((384, 384), BF16)] * 2 + [pltpu.VMEM((384, 128), F32)]
        + [pltpu.VMEM((2, 480, 256), F32), pltpu.VMEM((192, 256), F32), pltpu.VMEM((5, 384, 256), BF16)]
        + [pltpu.VMEM((8, 5, 64, 384), F32), pltpu.SemaphoreType.DMA((8,))],
        cost_estimate=pl.CostEstimate(flops=10**9, bytes_accessed=1000, transcendentals=0),
        compiler_params=pltpu.CompilerParams(vmem_limit_bytes=52 * 1024 * 1024),
    )(par.reshape(1), both, *ordered, mark)
    half = keep + lax.ppermute(send, "par", [(0, 1), (1, 0)])
    got = lax.all_to_all(half.reshape(32, 1, 2304), ("y", "zh", "pair"), 0, 0, tiled=True).reshape(576, 128)
    r = ((x * 4 + y) * 2 + zh) * 2 + core
    place = jnp.stack([x, core, r * 3, (pair * 2 + par) * 5, window_start[0], par])
    new, inc = call(
        final_kernel, 3, 3, [(5, 3, 1152)] * 2,
        [pltpu.VMEM((192, 128), F32), pltpu.VMEM((3, 1152), F32), pltpu.VMEM((3, 1152), F32)],
    )(place, occupied_energy, virtual_energy, got, virtual_energy.reshape(1, 192), res)
    return jnp.transpose(new, (1, 0, 2)), jnp.transpose(inc, (1, 0, 2))


def solution(mesh):
    fine = Mesh(mesh.devices.reshape(SIZES), AXES)
    split = P(("x", "y", "zh", "core"), ("pair", "par"), None)
    return jax.shard_map(
        body, mesh=fine, in_specs=(split, split, split, P(), P(), P()), out_specs=(split, split), check_vma=False
    )
```

```python
import jax
import jax.numpy as jnp
from jax import lax
from jax.experimental import pallas as pl
from jax.experimental.pallas import tpu as pltpu
from jax.sharding import Mesh, PartitionSpec as P

AXES = ("x", "y", "zh", "core", "pair", "par")
SIZES = (4, 4, 2, 2, 4, 2)
F32, BF16 = jnp.float32, jnp.bfloat16
VMEM = pl.BlockSpec(memory_space=pltpu.VMEM)
SMEM = pl.BlockSpec(memory_space=pltpu.SMEM)
NT = (((1,), (1,)), ((), ()))
NN = (((1,), (0,)), ((), ()))


def index(shape, axis):
    return lax.broadcasted_iota(jnp.int32, shape, axis)


def third(n, count):
    return sum((n >= 3 * s).astype(jnp.int32) for s in range(1, count))


def hot(mask):
    return jnp.where(mask, 1.0, 0.0).astype(BF16)


def order_matrix(e):
    n = index((1, 384), 1)
    source = (n * 10923) >> 16
    m = n - source * 6 - e * 3
    v = ((source >> 2) & 3) * 48 + (source >> 4) * 12 + ((source >> 1) & 1) * 6 + (source & 1) * 3 + m
    v = jnp.where((m >= 0) & (m < 3), v, -1)
    return hot(index((256, 384), 0) == v)


def choose_matrix():
    n = index((1, 256), 1)
    block = sum((n >= 24 * s).astype(jnp.int32) for s in range(1, 11))
    q = n - block * 24
    yz = third(q, 8)
    v = (block >> 1) * 48 + (block & 1) * 3 + yz * 6 + q - yz * 3
    v = jnp.where(block < 8, v, -1)
    return hot(index((256, 256), 0) == v)


def turn_matrix():
    n = index((1, 384), 1)
    p, q = n >> 7, n & 127
    k = sum((q >= 24 * s).astype(jnp.int32) for s in range(1, 6))
    q = q - k * 24
    yz = third(q, 8)
    row = k * 96 + (yz >> 1) * 24 + (yz & 1) * 9 + p * 3 + q - yz * 3
    row = jnp.where(k < 5, row, -1)
    return hot(index((480, 384), 0) == row)


def spread_matrix(par):
    n = index((1, 1280), 1)
    j, q = n >> 8, n & 255
    slot = jnp.where((j & 1) == par, (j - par) >> 1, (j >> 1) + 3 - par)
    x = sum((q >= 48 * s).astype(jnp.int32) for s in range(1, 6))
    q = q - x * 48
    core = third(q, 2)
    row = (x * 2 + core) * 16 + slot * 3 + q - core * 3
    row = jnp.where((x < 4) & (q < 6), row, -1)
    return hot(index((128, 1280), 0) == row)


def dot(a, b, dims=NN):
    return lax.dot_general(a, b, dims, preferred_element_type=F32)


def split2(v):
    high = v.astype(BF16)
    return high, (v - high.astype(F32)).astype(BF16)


def moved(v, hot):
    high = v.astype(BF16)
    rest = v - high.astype(F32)
    mid = rest.astype(BF16)
    low = (rest - mid.astype(F32)).astype(BF16)
    return (dot(low, hot) + dot(mid, hot)) + dot(high, hot)


def weights_kernel(ints_ref, token_ref, out_ref):
    out_ref[...] = jnp.zeros_like(out_ref)
    for k in range(5):
        for n in range(20):
            at = n // 5 * 16 + n % 5 * 3
            out_ref[k, at:at + 3, :] = ints_ref[k, :, n * 384:(n + 1) * 384]


def swap_kernel(own_ref, two_ref, rows):
    rows[...] = jnp.zeros_like(rows)
    for k in range(5):
        for p in range(3):
            v = own_ref[k, :, p * 384:(p + 1) * 384]
            at = k * 24 + p * 6
            rows[at:at + 3, :] = v[:, :256]
            rows[at + 3:at + 6, :] = pltpu.roll(v[:, 128:], 192, 1)
    chosen = moved(rows[...], choose_matrix())
    lane = index((24, 128), 1)
    for n in range(8):
        part = jnp.zeros((24, 128), F32)
        for k in range(5):
            v = pltpu.roll(chosen[k * 24:(k + 1) * 24, :], (k * 24 - n * 24) % 256, 1)[:, :128]
            part = jnp.where((lane >= k * 24) & (lane < k * 24 + 24), v, part)
        for zh in range(2):
            two_ref[n // 2 * 4 + zh * 2 + n % 2] = part


def merge_kernel(zh_ref, own_ref, other_ref, out_ref, rows):
    first = zh_ref[0] == 0
    rows[...] = jnp.zeros_like(rows)
    for k in range(5):
        for p in range(3):
            own = own_ref[k, :, p * 384:(p + 1) * 384]
            other = other_ref[k, :, p * 384:(p + 1) * 384]
            at = k * 18 + p * 3
            rows[at:at + 3, :] = jnp.where(first, own, other)
            rows[at + 9:at + 12, :] = jnp.where(first, other, own)
    for part in range(3):
        out_ref[part * 96:(part + 1) * 96, :] = rows[:, part * 128:(part + 1) * 128]


def pack_kernel(one_ref, two_ref, out_ref):
    for y in range(4):
        out_ref[y, :288, :] = one_ref[...]
        for n in range(16):
            out_ref[y, 288 + n * 18:306 + n * 18, :] = two_ref[n, :18, :]


def mark_kernel(*refs):
    refs[-1][...] = jnp.zeros_like(refs[-1])


def product_kernel(par_ref, got_ref, *refs):
    weights, (keep_ref, send_ref) = refs[:8], refs[10:12]
    two_high, two_low, stage, swapped, whole, mixed = refs[12:]
    for p in range(3):
        for y in range(4):
            for n in range(16):
                at = 288 + n * 18 + p * 6
                stage[y * 96 + n * 6:y * 96 + n * 6 + 6, :] = got_ref[y, at:at + 6, :]
        high, low = split2(stage[...])
        two_high[:, p * 128:(p + 1) * 128] = high
        two_low[:, p * 128:(p + 1) * 128] = low
    turn = turn_matrix()
    parts = [dot(turn, two[...], NT).astype(BF16) for two in (two_high, two_low)]
    parts = jnp.concatenate(parts, 0)
    for e in range(2):
        moved_parts = dot(parts, order_matrix(e), NT)
        swapped[e] = moved_parts[:480] + moved_parts[480:]
    lane = index((24, 256), 1)
    for k in range(5):
        for y in range(4):
            v = [got_ref[y, part * 96 + k * 18:part * 96 + k * 18 + 24, :] for part in range(3)]
            near = jnp.concatenate(v[:2], 1)
            far = pltpu.roll(jnp.concatenate(v[1:], 1), 192, 1)
            for e, straight in enumerate((near, far)):
                at = (k * 4 + y) * 24
                value = 2.0 * jnp.where(lane < 192, straight, 0.0) - swapped[e, at:at + 24, :]
                whole[y * 48 + e * 24:y * 48 + e * 24 + 24, :] = value
        high, low = split2(whole[...])
        mixed[k, :192] = high
        mixed[k, 192:] = low
    even = par_ref[0] == 0
    slot = index((192, 128), 1) & 15
    for q in range(4):
        total = jnp.zeros((192, 256), F32)
        for k in range(5):
            rows = [ref[k, q * 16:(q + 1) * 16, :] for ref in weights]
            near = [v[:, :256] for v in rows]
            far = [pltpu.roll(v[:, 128:], 192, 1) for v in rows]
            high, low = split2(jnp.concatenate(near + far, 0))
            both = dot(mixed[k], high, NT)
            total += dot(mixed[k, :192], low, NT) + both[192:]
            total += both[:192]
        near, far = total[:, :128], total[:, 128:]
        first = jnp.where(slot < 9, near, pltpu.roll(far, 9, 1))
        second = jnp.where(slot < 6, pltpu.roll(near, 119, 1), far)
        for ref, v in ((keep_ref, jnp.where(even, first, second)), (send_ref, jnp.where(even, second, first))):
            for yz in range(8):
                for e in range(2):
                    to = (yz * 4 + q) * 18 + e * 9
                    at = yz // 2 * 48 + e * 24 + yz % 2 * 9
                    ref[to:to + 9, :] = v[at:at + 9, :]


def final_kernel(place_ref, occ_ref, va_ref, got_ref, vb_ref, res_ref, new_ref, inc_ref, sums, cyc, den):
    sums[...] = jnp.zeros_like(sums)
    for yz in range(8):
        total = got_ref[yz * 72:yz * 72 + 18, :]
        for z in range(1, 4):
            at = (yz * 4 + z) * 18
            total += got_ref[at:at + 18, :]
        sums[yz * 24:yz * 24 + 18, :] = total
    v = pltpu.roll(sums[...], place_ref[0] * 32, 1)
    lane = lax.broadcasted_iota(jnp.int32, v.shape, 1)
    other = jnp.where((lane & 16) == 0, pltpu.roll(v, 112, 1), pltpu.roll(v, 16, 1))
    v = jnp.where(place_ref[1] == 0, v, other)
    wide = moved(v, spread_matrix(place_ref[5]))
    row = lax.broadcasted_iota(jnp.int32, (3, 192), 0)
    va = [va_ref[place_ref[2] + m] for m in range(3)]
    va = jnp.where(row == 0, va[0], jnp.where(row == 1, va[1], va[2]))
    base = vb_ref[...] + va
    for i in range(6):
        den[:, i * 192:(i + 1) * 192] = base - occ_ref[place_ref[4] + i]
    for j in range(5):
        total = wide[0:24, j * 256:(j + 1) * 256]
        for yz in range(1, 8):
            total += pltpu.roll(wide[yz * 24:(yz + 1) * 24, j * 256:(j + 1) * 256], yz * 6, 1)
        for i in range(6):
            cyc[:, i * 192:(i + 1) * 192] = total[i % 2 * 9 + i // 2 * 3:i % 2 * 9 + i // 2 * 3 + 3, :192]
        new = res_ref[j] + cyc[...]
        new_ref[j] = new
        inc_ref[j] = new / (den[...] - occ_ref[place_ref[3] + j])


def call(kernel, n_smem, n_vmem, outs, scratch, mib=8, dtype=F32, cost=1000, space=pltpu.VMEM):
    shapes = [jax.ShapeDtypeStruct(s, dtype) for s in outs]
    return pl.pallas_call(
        kernel,
        out_shape=shapes if len(shapes) > 1 else shapes[0],
        in_specs=[SMEM] * n_smem + [pl.BlockSpec(memory_space=space)] * n_vmem,
        out_specs=[VMEM] * len(shapes) if len(shapes) > 1 else VMEM,
        scratch_shapes=scratch,
        cost_estimate=pl.CostEstimate(flops=cost * 10**6, bytes_accessed=1000, transcendentals=0),
        compiler_params=pltpu.CompilerParams(vmem_limit_bytes=mib * 1024 * 1024),
    )


def body(amplitudes, integrals, residual, occupied_energy, virtual_energy, window_start):
    x, y, zh, core, pair, par = [lax.axis_index(a).astype(jnp.int32) for a in AXES]
    amps = jnp.transpose(amplitudes, (1, 0, 2))
    ints = jnp.transpose(integrals, (1, 0, 2))
    res = jnp.transpose(residual, (1, 0, 2))
    other = lax.ppermute(amps, "zh", [(0, 1), (1, 0)])
    two = call(swap_kernel, 0, 1, [(16, 24, 128)], [pltpu.VMEM((120, 256), F32)])(amps)
    weights = call(weights_kernel, 0, 2, [(5, 64, 384)], [])(ints, two)
    along = [weights] + [
        lax.ppermute(weights, "x", [(s, (s - d) % 4) for s in range(4)]) for d in (1, 3, 2)
    ]
    across = [lax.ppermute(w, "core", [(0, 1), (1, 0)]) for w in along]
    two = lax.all_to_all(two, ("x", "zh", "core"), 0, 0, tiled=True)
    one = call(merge_kernel, 1, 2, [(288, 128)], [pltpu.VMEM((96, 384), F32)], cost=8000)(zh.reshape(1), amps, other)
    both = call(pack_kernel, 0, 2, [(4, 576, 128)], [])(one, two)
    both = lax.all_to_all(both, "y", 0, 0, tiled=True)
    ordered = [w for pair in zip(along, across) for w in pair]
    ordered = ordered[:4] + ordered[6:] + ordered[4:6]
    mark = call(mark_kernel, 0, 4, [(8, 128)], [], 8, F32, 5000, pl.ANY)(*along)
    wait = call(mark_kernel, 0, 1, [(8, 128)], [], 8, F32, 1000, pl.ANY)(both)
    keep, send = pl.pallas_call(
        product_kernel,
        out_shape=[jax.ShapeDtypeStruct((576, 128), F32)] * 2,
        in_specs=[SMEM] + [VMEM] * 9 + [pl.BlockSpec(memory_space=pl.ANY)] * 2,
        out_specs=[VMEM] * 2,
        scratch_shapes=[pltpu.VMEM((384, 384), BF16)] * 2 + [pltpu.VMEM((384, 128), F32)]
        + [pltpu.VMEM((2, 480, 256), F32), pltpu.VMEM((192, 256), F32), pltpu.VMEM((5, 384, 256), BF16)],
        cost_estimate=pl.CostEstimate(flops=10**9, bytes_accessed=1000, transcendentals=0),
        compiler_params=pltpu.CompilerParams(vmem_limit_bytes=24 * 1024 * 1024),
    )(par.reshape(1), both, *ordered, mark, wait)
    half = keep + lax.ppermute(send, "par", [(0, 1), (1, 0)])
    got = lax.all_to_all(half.reshape(32, 1, 2304), ("y", "zh", "pair"), 0, 0, tiled=True).reshape(576, 128)
    r = ((x * 4 + y) * 2 + zh) * 2 + core
    place = jnp.stack([x, core, r * 3, (pair * 2 + par) * 5, window_start[0], par])
    new, inc = call(
        final_kernel, 3, 3, [(5, 3, 1152)] * 2,
        [pltpu.VMEM((192, 128), F32), pltpu.VMEM((3, 1152), F32), pltpu.VMEM((3, 1152), F32)],
    )(place, occupied_energy, virtual_energy, got, virtual_energy.reshape(1, 192), res)
    return jnp.transpose(new, (1, 0, 2)), jnp.transpose(inc, (1, 0, 2))


def solution(mesh):
    fine = Mesh(mesh.devices.reshape(SIZES), AXES)
    split = P(("x", "y", "zh", "core"), ("pair", "par"), None)
    return jax.shard_map(
        body, mesh=fine, in_specs=(split, split, split, P(), P(), P()), out_specs=(split, split), check_vma=False
    )
```

```python
import jax
import jax.numpy as jnp
from jax import lax
from jax.experimental import pallas as pl
from jax.experimental.pallas import tpu as pltpu
from jax.sharding import Mesh, PartitionSpec as P

AXES = ("x", "y", "zh", "core", "pair", "par")
SIZES = (4, 4, 2, 2, 4, 2)
F32, BF16 = jnp.float32, jnp.bfloat16
VMEM = pl.BlockSpec(memory_space=pltpu.VMEM)
SMEM = pl.BlockSpec(memory_space=pltpu.SMEM)
NT = (((1,), (1,)), ((), ()))
NN = (((1,), (0,)), ((), ()))


def index(shape, axis):
    return lax.broadcasted_iota(jnp.int32, shape, axis)


def third(n, count):
    return sum((n >= 3 * s).astype(jnp.int32) for s in range(1, count))


def hot(mask):
    return jnp.where(mask, 1.0, 0.0).astype(BF16)


def order_matrix(e):
    n = index((1, 384), 1)
    source = (n * 10923) >> 16
    m = n - source * 6 - e * 3
    v = ((source >> 2) & 3) * 48 + (source >> 4) * 12 + ((source >> 1) & 1) * 6 + (source & 1) * 3 + m
    v = jnp.where((m >= 0) & (m < 3), v, -1)
    return hot(index((256, 384), 0) == v)


def choose_matrix():
    n = index((1, 256), 1)
    block = sum((n >= 24 * s).astype(jnp.int32) for s in range(1, 11))
    q = n - block * 24
    yz = third(q, 8)
    v = (block >> 1) * 48 + (block & 1) * 3 + yz * 6 + q - yz * 3
    v = jnp.where(block < 8, v, -1)
    return hot(index((256, 256), 0) == v)


def turn_matrix():
    n = index((1, 384), 1)
    p, q = n >> 7, n & 127
    k = sum((q >= 24 * s).astype(jnp.int32) for s in range(1, 6))
    q = q - k * 24
    yz = third(q, 8)
    row = k * 96 + (yz >> 1) * 24 + (yz & 1) * 9 + p * 3 + q - yz * 3
    row = jnp.where(k < 5, row, -1)
    return hot(index((480, 384), 0) == row)


def spread_matrix(par):
    n = index((1, 1280), 1)
    j, q = n >> 8, n & 255
    slot = jnp.where((j & 1) == par, (j - par) >> 1, (j >> 1) + 3 - par)
    x = sum((q >= 48 * s).astype(jnp.int32) for s in range(1, 6))
    q = q - x * 48
    core = third(q, 2)
    row = (x * 2 + core) * 16 + slot * 3 + q - core * 3
    row = jnp.where((x < 4) & (q < 6), row, -1)
    return hot(index((128, 1280), 0) == row)


def dot(a, b, dims=NN):
    return lax.dot_general(a, b, dims, preferred_element_type=F32)


def split2(v):
    high = v.astype(BF16)
    return high, (v - high.astype(F32)).astype(BF16)


def moved(v, hot):
    high = v.astype(BF16)
    rest = v - high.astype(F32)
    mid = rest.astype(BF16)
    low = (rest - mid.astype(F32)).astype(BF16)
    return (dot(low, hot) + dot(mid, hot)) + dot(high, hot)


def weights_kernel(ints_ref, token_ref, out_ref):
    out_ref[...] = jnp.zeros_like(out_ref)
    for k in range(5):
        for n in range(20):
            at = n // 5 * 16 + n % 5 * 3
            out_ref[k, at:at + 3, :] = ints_ref[k, :, n * 384:(n + 1) * 384]


def swap_kernel(own_ref, two_ref, rows):
    rows[...] = jnp.zeros_like(rows)
    for k in range(5):
        for p in range(3):
            v = own_ref[k, :, p * 384:(p + 1) * 384]
            at = k * 24 + p * 6
            rows[at:at + 3, :] = v[:, :256]
            rows[at + 3:at + 6, :] = pltpu.roll(v[:, 128:], 192, 1)
    chosen = moved(rows[...], choose_matrix())
    lane = index((24, 128), 1)
    for n in range(8):
        part = jnp.zeros((24, 128), F32)
        for k in range(5):
            v = pltpu.roll(chosen[k * 24:(k + 1) * 24, :], (k * 24 - n * 24) % 256, 1)[:, :128]
            part = jnp.where((lane >= k * 24) & (lane < k * 24 + 24), v, part)
        for zh in range(2):
            two_ref[n // 2 * 4 + zh * 2 + n % 2] = part


def merge_kernel(zh_ref, own_ref, other_ref, out_ref, rows):
    first = zh_ref[0] == 0
    rows[...] = jnp.zeros_like(rows)
    for k in range(5):
        for p in range(3):
            own = own_ref[k, :, p * 384:(p + 1) * 384]
            other = other_ref[k, :, p * 384:(p + 1) * 384]
            at = k * 18 + p * 3
            rows[at:at + 3, :] = jnp.where(first, own, other)
            rows[at + 9:at + 12, :] = jnp.where(first, other, own)
    for part in range(3):
        out_ref[part * 96:(part + 1) * 96, :] = rows[:, part * 128:(part + 1) * 128]


def pack_kernel(one_ref, two_ref, out_ref):
    for y in range(4):
        out_ref[y, :288, :] = one_ref[...]
        for n in range(16):
            out_ref[y, 288 + n * 18:306 + n * 18, :] = two_ref[n, :18, :]


def mark_kernel(*refs):
    refs[-1][...] = jnp.zeros_like(refs[-1])


def product_kernel(par_ref, got_ref, *refs):
    weights, (keep_ref, send_ref) = refs[:8], refs[10:12]
    two_high, two_low, stage, swapped, whole, mixed = refs[12:]
    for p in range(3):
        for y in range(4):
            for n in range(16):
                at = 288 + n * 18 + p * 6
                stage[y * 96 + n * 6:y * 96 + n * 6 + 6, :] = got_ref[y, at:at + 6, :]
        high, low = split2(stage[...])
        two_high[:, p * 128:(p + 1) * 128] = high
        two_low[:, p * 128:(p + 1) * 128] = low
    turn = turn_matrix()
    parts = [dot(turn, two[...], NT).astype(BF16) for two in (two_high, two_low)]
    parts = jnp.concatenate(parts, 0)
    for e in range(2):
        moved_parts = dot(parts, order_matrix(e), NT)
        swapped[e] = moved_parts[:480] + moved_parts[480:]
    lane = index((24, 256), 1)
    for k in range(5):
        for y in range(4):
            v = [got_ref[y, part * 96 + k * 18:part * 96 + k * 18 + 24, :] for part in range(3)]
            near = jnp.concatenate(v[:2], 1)
            far = pltpu.roll(jnp.concatenate(v[1:], 1), 192, 1)
            for e, straight in enumerate((near, far)):
                at = (k * 4 + y) * 24
                value = 2.0 * jnp.where(lane < 192, straight, 0.0) - swapped[e, at:at + 24, :]
                whole[y * 48 + e * 24:y * 48 + e * 24 + 24, :] = value
        high, low = split2(whole[...])
        mixed[k, :192] = high
        mixed[k, 192:] = low
    even = par_ref[0] == 0
    slot = index((192, 128), 1) & 15
    for q in range(4):
        total = jnp.zeros((192, 256), F32)
        for k in range(5):
            rows = [ref[k, q * 16:(q + 1) * 16, :] for ref in weights]
            near = [v[:, :256] for v in rows]
            far = [pltpu.roll(v[:, 128:], 192, 1) for v in rows]
            high, low = split2(jnp.concatenate(near + far, 0))
            both = dot(mixed[k], high, NT)
            total += dot(mixed[k, :192], low, NT) + both[192:]
            total += both[:192]
        near, far = total[:, :128], total[:, 128:]
        first = jnp.where(slot < 9, near, pltpu.roll(far, 9, 1))
        second = jnp.where(slot < 6, pltpu.roll(near, 119, 1), far)
        for ref, v in ((keep_ref, jnp.where(even, first, second)), (send_ref, jnp.where(even, second, first))):
            for yz in range(8):
                for e in range(2):
                    to = (yz * 4 + q) * 18 + e * 9
                    at = yz // 2 * 48 + e * 24 + yz % 2 * 9
                    ref[to:to + 9, :] = v[at:at + 9, :]


def spread_kernel(place_ref, out_ref):
    out_ref[...] = spread_matrix(place_ref[5])


def denominator_kernel(place_ref, occ_ref, va_ref, vb_ref, out_ref):
    row = index((3, 192), 0)
    va = [va_ref[place_ref[2] + m] for m in range(3)]
    va = jnp.where(row == 0, va[0], jnp.where(row == 1, va[1], va[2]))
    base = vb_ref[...] + va
    for j in range(5):
        for i in range(6):
            out_ref[j, :, i * 192:(i + 1) * 192] = base - occ_ref[place_ref[4] + i] - occ_ref[place_ref[3] + j]


def final_kernel(place_ref, got_ref, spread_ref, den_ref, res_ref, new_ref, inc_ref, sums, cyc):
    sums[...] = jnp.zeros_like(sums)
    for yz in range(8):
        total = got_ref[yz * 72:yz * 72 + 18, :]
        for z in range(1, 4):
            at = (yz * 4 + z) * 18
            total += got_ref[at:at + 18, :]
        sums[yz * 24:yz * 24 + 18, :] = total
    v = pltpu.roll(sums[...], place_ref[0] * 32, 1)
    lane = index(v.shape, 1)
    other = jnp.where((lane & 16) == 0, pltpu.roll(v, 112, 1), pltpu.roll(v, 16, 1))
    v = jnp.where(place_ref[1] == 0, v, other)
    wide = moved(v, spread_ref[...])
    for j in range(5):
        total = wide[0:24, j * 256:(j + 1) * 256]
        for yz in range(1, 8):
            total += pltpu.roll(wide[yz * 24:(yz + 1) * 24, j * 256:(j + 1) * 256], yz * 6, 1)
        for i in range(6):
            at = i % 2 * 9 + i // 2 * 3
            cyc[:, i * 192:(i + 1) * 192] = total[at:at + 3, :192]
        new = res_ref[j] + cyc[...]
        new_ref[j] = new
        inc_ref[j] = new / den_ref[j]


def call(kernel, n_smem, n_vmem, outs, scratch, mib=8, dtype=F32, cost=1000, space=pltpu.VMEM):
    shapes = [jax.ShapeDtypeStruct(s, dtype) for s in outs]
    return pl.pallas_call(
        kernel,
        out_shape=shapes if len(shapes) > 1 else shapes[0],
        in_specs=[SMEM] * n_smem + [pl.BlockSpec(memory_space=space)] * n_vmem,
        out_specs=[VMEM] * len(shapes) if len(shapes) > 1 else VMEM,
        scratch_shapes=scratch,
        cost_estimate=pl.CostEstimate(flops=cost * 10**6, bytes_accessed=1000, transcendentals=0),
        compiler_params=pltpu.CompilerParams(vmem_limit_bytes=mib * 1024 * 1024),
    )


def body(amplitudes, integrals, residual, occupied_energy, virtual_energy, window_start):
    x, y, zh, core, pair, par = [lax.axis_index(a).astype(jnp.int32) for a in AXES]
    amps = jnp.transpose(amplitudes, (1, 0, 2))
    ints = jnp.transpose(integrals, (1, 0, 2))
    res = jnp.transpose(residual, (1, 0, 2))
    other = lax.ppermute(amps, "zh", [(0, 1), (1, 0)])
    two = call(swap_kernel, 0, 1, [(16, 24, 128)], [pltpu.VMEM((120, 256), F32)])(amps)
    weights = call(weights_kernel, 0, 2, [(5, 64, 384)], [])(ints, two)
    along = [weights] + [
        lax.ppermute(weights, "x", [(s, (s - d) % 4) for s in range(4)]) for d in (1, 3, 2)
    ]
    across = [lax.ppermute(w, "core", [(0, 1), (1, 0)]) for w in along]
    two = lax.all_to_all(two, ("x", "zh", "core"), 0, 0, tiled=True)
    one = call(merge_kernel, 1, 2, [(288, 128)], [pltpu.VMEM((96, 384), F32)], cost=8000)(zh.reshape(1), amps, other)
    both = call(pack_kernel, 0, 2, [(4, 576, 128)], [])(one, two)
    both = lax.all_to_all(both, "y", 0, 0, tiled=True)
    ordered = [w for pair in zip(along, across) for w in pair]
    ordered = ordered[:4] + ordered[6:] + ordered[4:6]
    mark = call(mark_kernel, 0, 4, [(8, 128)], [], 8, F32, 5000, pl.ANY)(*along)
    wait = call(mark_kernel, 0, 1, [(8, 128)], [], 8, F32, 1000, pl.ANY)(both)
    keep, send = pl.pallas_call(
        product_kernel,
        out_shape=[jax.ShapeDtypeStruct((576, 128), F32)] * 2,
        in_specs=[SMEM] + [VMEM] * 9 + [pl.BlockSpec(memory_space=pl.ANY)] * 2,
        out_specs=[VMEM] * 2,
        scratch_shapes=[pltpu.VMEM((384, 384), BF16)] * 2 + [pltpu.VMEM((384, 128), F32)]
        + [pltpu.VMEM((2, 480, 256), F32), pltpu.VMEM((192, 256), F32), pltpu.VMEM((5, 384, 256), BF16)],
        cost_estimate=pl.CostEstimate(flops=10**9, bytes_accessed=1000, transcendentals=0),
        compiler_params=pltpu.CompilerParams(vmem_limit_bytes=24 * 1024 * 1024),
    )(par.reshape(1), both, *ordered, mark, wait)
    half = keep + lax.ppermute(send, "par", [(0, 1), (1, 0)])
    got = lax.all_to_all(half.reshape(32, 1, 2304), ("y", "zh", "pair"), 0, 0, tiled=True).reshape(576, 128)
    r = ((x * 4 + y) * 2 + zh) * 2 + core
    place = jnp.stack([x, core, r * 3, (pair * 2 + par) * 5, window_start[0], par])
    spread = call(spread_kernel, 1, 0, [(128, 1280)], [], 8, BF16)(place)
    den = call(denominator_kernel, 3, 1, [(5, 3, 1152)], [])(
        place, occupied_energy, virtual_energy, virtual_energy.reshape(1, 192)
    )
    new, inc = call(
        final_kernel, 1, 4, [(5, 3, 1152)] * 2, [pltpu.VMEM((192, 128), F32), pltpu.VMEM((3, 1152), F32)]
    )(place, got, spread, den, res)
    return jnp.transpose(new, (1, 0, 2)), jnp.transpose(inc, (1, 0, 2))


def solution(mesh):
    fine = Mesh(mesh.devices.reshape(SIZES), AXES)
    split = P(("x", "y", "zh", "core"), ("pair", "par"), None)
    return jax.shard_map(
        body, mesh=fine, in_specs=(split, split, split, P(), P(), P()), out_specs=(split, split), check_vma=False
    )
```

```python
import jax
import jax.numpy as jnp
from jax import lax
from jax.experimental import pallas as pl
from jax.experimental.pallas import tpu as pltpu
from jax.sharding import Mesh, PartitionSpec as P

AXES = ("x", "y", "zh", "core", "pair", "par")
SIZES = (4, 4, 2, 2, 4, 2)
F32, BF16 = jnp.float32, jnp.bfloat16
VMEM = pl.BlockSpec(memory_space=pltpu.VMEM)
SMEM = pl.BlockSpec(memory_space=pltpu.SMEM)
NT = (((1,), (1,)), ((), ()))
NN = (((1,), (0,)), ((), ()))


def index(shape, axis):
    return lax.broadcasted_iota(jnp.int32, shape, axis)


def third(n, count):
    return sum((n >= 3 * s).astype(jnp.int32) for s in range(1, count))


def hot(mask):
    return jnp.where(mask, 1.0, 0.0).astype(BF16)


def order_matrix(e):
    n = index((1, 384), 1)
    source = (n * 10923) >> 16
    m = n - source * 6 - e * 3
    v = ((source >> 2) & 3) * 48 + (source >> 4) * 12 + ((source >> 1) & 1) * 6 + (source & 1) * 3 + m
    v = jnp.where((m >= 0) & (m < 3), v, -1)
    return hot(index((256, 384), 0) == v)


def choose_matrix():
    n = index((1, 256), 1)
    block = sum((n >= 24 * s).astype(jnp.int32) for s in range(1, 11))
    q = n - block * 24
    yz = third(q, 8)
    v = (block >> 1) * 48 + (block & 1) * 3 + yz * 6 + q - yz * 3
    v = jnp.where(block < 8, v, -1)
    return hot(index((256, 256), 0) == v)


def turn_matrix():
    n = index((1, 384), 1)
    p, q = n >> 7, n & 127
    k = sum((q >= 24 * s).astype(jnp.int32) for s in range(1, 6))
    q = q - k * 24
    yz = third(q, 8)
    row = k * 96 + (yz >> 1) * 24 + (yz & 1) * 9 + p * 3 + q - yz * 3
    row = jnp.where(k < 5, row, -1)
    return hot(index((480, 384), 0) == row)


def spread_matrix(par):
    n = index((1, 1280), 1)
    j, q = n >> 8, n & 255
    slot = jnp.where((j & 1) == par, (j - par) >> 1, (j >> 1) + 3 - par)
    x = sum((q >= 48 * s).astype(jnp.int32) for s in range(1, 6))
    q = q - x * 48
    core = third(q, 2)
    row = (x * 2 + core) * 16 + slot * 3 + q - core * 3
    row = jnp.where((x < 4) & (q < 6), row, -1)
    return hot(index((128, 1280), 0) == row)


def dot(a, b, dims=NN):
    return lax.dot_general(a, b, dims, preferred_element_type=F32)


def split2(v):
    high = v.astype(BF16)
    return high, (v - high.astype(F32)).astype(BF16)


def moved(v, hot):
    high = v.astype(BF16)
    rest = v - high.astype(F32)
    mid = rest.astype(BF16)
    low = (rest - mid.astype(F32)).astype(BF16)
    return (dot(low, hot) + dot(mid, hot)) + dot(high, hot)


def weights_kernel(ints_ref, token_ref, out_ref):
    out_ref[...] = jnp.zeros_like(out_ref)
    for k in range(5):
        for n in range(20):
            at = n // 5 * 16 + n % 5 * 3
            out_ref[k, at:at + 3, :] = ints_ref[k, :, n * 384:(n + 1) * 384]


def swap_kernel(own_ref, two_ref, rows):
    rows[...] = jnp.zeros_like(rows)
    for k in range(5):
        for p in range(3):
            v = own_ref[k, :, p * 384:(p + 1) * 384]
            at = k * 24 + p * 6
            rows[at:at + 3, :] = v[:, :256]
            rows[at + 3:at + 6, :] = pltpu.roll(v[:, 128:], 192, 1)
    chosen = moved(rows[...], choose_matrix())
    lane = index((24, 128), 1)
    for n in range(8):
        part = jnp.zeros((24, 128), F32)
        for k in range(5):
            v = pltpu.roll(chosen[k * 24:(k + 1) * 24, :], (k * 24 - n * 24) % 256, 1)[:, :128]
            part = jnp.where((lane >= k * 24) & (lane < k * 24 + 24), v, part)
        for zh in range(2):
            two_ref[n // 2 * 4 + zh * 2 + n % 2] = part


def merge_kernel(zh_ref, own_ref, other_ref, out_ref, rows):
    first = zh_ref[0] == 0
    rows[...] = jnp.zeros_like(rows)
    for k in range(5):
        for p in range(3):
            own = own_ref[k, :, p * 384:(p + 1) * 384]
            other = other_ref[k, :, p * 384:(p + 1) * 384]
            at = k * 18 + p * 3
            rows[at:at + 3, :] = jnp.where(first, own, other)
            rows[at + 9:at + 12, :] = jnp.where(first, other, own)
    for part in range(3):
        out_ref[part * 96:(part + 1) * 96, :] = rows[:, part * 128:(part + 1) * 128]


def pack_kernel(one_ref, two_ref, out_ref):
    for y in range(4):
        out_ref[y, :288, :] = one_ref[...]
        for n in range(16):
            out_ref[y, 288 + n * 18:306 + n * 18, :] = two_ref[n, :18, :]


def mark_kernel(*refs):
    refs[-1][...] = jnp.zeros_like(refs[-1])


def product_kernel(par_ref, got_ref, *refs):
    weights, (keep_ref, send_ref) = refs[:8], refs[10:12]
    two_high, two_low, stage, swapped, whole, mixed = refs[12:]
    for p in range(3):
        for y in range(4):
            for n in range(16):
                at = 288 + n * 18 + p * 6
                stage[y * 96 + n * 6:y * 96 + n * 6 + 6, :] = got_ref[y, at:at + 6, :]
        high, low = split2(stage[...])
        two_high[:, p * 128:(p + 1) * 128] = high
        two_low[:, p * 128:(p + 1) * 128] = low
    turn = turn_matrix()
    parts = [dot(turn, two[...], NT).astype(BF16) for two in (two_high, two_low)]
    parts = jnp.concatenate(parts, 0)
    for e in range(2):
        moved_parts = dot(parts, order_matrix(e), NT)
        swapped[e] = moved_parts[:480] + moved_parts[480:]
    lane = index((24, 256), 1)
    for k in range(5):
        for y in range(4):
            v = [got_ref[y, part * 96 + k * 18:part * 96 + k * 18 + 24, :] for part in range(3)]
            near = jnp.concatenate(v[:2], 1)
            far = pltpu.roll(jnp.concatenate(v[1:], 1), 192, 1)
            for e, straight in enumerate((near, far)):
                at = (k * 4 + y) * 24
                value = 2.0 * jnp.where(lane < 192, straight, 0.0) - swapped[e, at:at + 24, :]
                whole[y * 48 + e * 24:y * 48 + e * 24 + 24, :] = value
        high, low = split2(whole[...])
        mixed[k, :192] = high
        mixed[k, 192:] = low
    even = par_ref[0] == 0
    slot = index((192, 128), 1) & 15
    for q in range(4):
        total = jnp.zeros((192, 256), F32)
        for k in range(5):
            rows = [ref[k, q * 16:(q + 1) * 16, :] for ref in weights]
            near = [v[:, :256] for v in rows]
            far = [pltpu.roll(v[:, 128:], 192, 1) for v in rows]
            high, low = split2(jnp.concatenate(near + far, 0))
            both = dot(mixed[k], high, NT)
            total += dot(mixed[k, :192], low, NT) + both[192:]
            total += both[:192]
        near, far = total[:, :128], total[:, 128:]
        first = jnp.where(slot < 9, near, pltpu.roll(far, 9, 1))
        second = jnp.where(slot < 6, pltpu.roll(near, 119, 1), far)
        for ref, v in ((keep_ref, jnp.where(even, first, second)), (send_ref, jnp.where(even, second, first))):
            for yz in range(8):
                for e in range(2):
                    to = (yz * 4 + q) * 18 + e * 9
                    at = yz // 2 * 48 + e * 24 + yz % 2 * 9
                    ref[to:to + 9, :] = v[at:at + 9, :]


def spread_kernel(place_ref, out_ref):
    out_ref[...] = spread_matrix(place_ref[5])


def denominator_kernel(place_ref, occ_ref, va_ref, vb_ref, out_ref):
    row = index((3, 192), 0)
    va = [va_ref[place_ref[2] + m] for m in range(3)]
    va = jnp.where(row == 0, va[0], jnp.where(row == 1, va[1], va[2]))
    base = vb_ref[...] + va
    for j in range(5):
        for i in range(6):
            out_ref[j, :, i * 192:(i + 1) * 192] = base - occ_ref[place_ref[4] + i] - occ_ref[place_ref[3] + j]


def final_kernel(place_ref, got_ref, spread_ref, den_ref, res_ref, new_ref, inc_ref, sums, cyc):
    sums[...] = jnp.zeros_like(sums)
    for yz in range(8):
        total = got_ref[yz * 72:yz * 72 + 18, :]
        for z in range(1, 4):
            at = (yz * 4 + z) * 18
            total += got_ref[at:at + 18, :]
        sums[yz * 24:yz * 24 + 18, :] = total
    v = pltpu.roll(sums[...], place_ref[0] * 32, 1)
    lane = index(v.shape, 1)
    other = jnp.where((lane & 16) == 0, pltpu.roll(v, 112, 1), pltpu.roll(v, 16, 1))
    v = jnp.where(place_ref[1] == 0, v, other)
    wide = moved(v, spread_ref[...])
    for j in range(5):
        total = wide[0:24, j * 256:(j + 1) * 256]
        for yz in range(1, 8):
            total += pltpu.roll(wide[yz * 24:(yz + 1) * 24, j * 256:(j + 1) * 256], yz * 6, 1)
        for i in range(6):
            at = i % 2 * 9 + i // 2 * 3
            cyc[:, i * 192:(i + 1) * 192] = total[at:at + 3, :192]
        new = res_ref[j] + cyc[...]
        new_ref[j] = new
        inc_ref[j] = new / den_ref[j]


def call(kernel, n_smem, n_vmem, outs, scratch, mib=8, dtype=F32, cost=1000, space=pltpu.VMEM):
    shapes = [jax.ShapeDtypeStruct(s, dtype) for s in outs]
    return pl.pallas_call(
        kernel,
        out_shape=shapes if len(shapes) > 1 else shapes[0],
        in_specs=[SMEM] * n_smem + [pl.BlockSpec(memory_space=space)] * n_vmem,
        out_specs=[VMEM] * len(shapes) if len(shapes) > 1 else VMEM,
        scratch_shapes=scratch,
        cost_estimate=pl.CostEstimate(flops=cost * 10**6, bytes_accessed=1000, transcendentals=0),
        compiler_params=pltpu.CompilerParams(vmem_limit_bytes=mib * 1024 * 1024),
    )


def body(amplitudes, integrals, residual, occupied_energy, virtual_energy, window_start):
    x, y, zh, core, pair, par = [lax.axis_index(a).astype(jnp.int32) for a in AXES]
    amps = jnp.transpose(amplitudes, (1, 0, 2))
    ints = jnp.transpose(integrals, (1, 0, 2))
    res = jnp.transpose(residual, (1, 0, 2))
    other = lax.ppermute(amps, "zh", [(0, 1), (1, 0)])
    two = call(swap_kernel, 0, 1, [(16, 24, 128)], [pltpu.VMEM((120, 256), F32)])(amps)
    weights = call(weights_kernel, 0, 2, [(5, 64, 384)], [])(ints, two)
    near, back = [lax.ppermute(weights, "x", [(s, (s - d) % 4) for s in range(4)]) for d in (1, 3)]
    along = [weights, near, back, lax.ppermute(near, "x", [(s, (s - 1) % 4) for s in range(4)])]
    across = [lax.ppermute(w, "core", [(0, 1), (1, 0)]) for w in along]
    two = lax.all_to_all(two, ("x", "zh", "core"), 0, 0, tiled=True)
    one = call(merge_kernel, 1, 2, [(288, 128)], [pltpu.VMEM((96, 384), F32)], cost=8000)(zh.reshape(1), amps, other)
    both = call(pack_kernel, 0, 2, [(4, 576, 128)], [])(one, two)
    both = lax.all_to_all(both, "y", 0, 0, tiled=True)
    ordered = [w for pair in zip(along, across) for w in pair]
    ordered = ordered[:4] + ordered[6:] + ordered[4:6]
    mark = call(mark_kernel, 0, 4, [(8, 128)], [], 8, F32, 5000, pl.ANY)(*along)
    wait = call(mark_kernel, 0, 1, [(8, 128)], [], 8, F32, 1000, pl.ANY)(both)
    keep, send = pl.pallas_call(
        product_kernel,
        out_shape=[jax.ShapeDtypeStruct((576, 128), F32)] * 2,
        in_specs=[SMEM] + [VMEM] * 9 + [pl.BlockSpec(memory_space=pl.ANY)] * 2,
        out_specs=[VMEM] * 2,
        scratch_shapes=[pltpu.VMEM((384, 384), BF16)] * 2 + [pltpu.VMEM((384, 128), F32)]
        + [pltpu.VMEM((2, 480, 256), F32), pltpu.VMEM((192, 256), F32), pltpu.VMEM((5, 384, 256), BF16)],
        cost_estimate=pl.CostEstimate(flops=10**9, bytes_accessed=1000, transcendentals=0),
        compiler_params=pltpu.CompilerParams(vmem_limit_bytes=24 * 1024 * 1024),
    )(par.reshape(1), both, *ordered, mark, wait)
    half = keep + lax.ppermute(send, "par", [(0, 1), (1, 0)])
    got = lax.all_to_all(half.reshape(32, 1, 2304), ("y", "zh", "pair"), 0, 0, tiled=True).reshape(576, 128)
    r = ((x * 4 + y) * 2 + zh) * 2 + core
    place = jnp.stack([x, core, r * 3, (pair * 2 + par) * 5, window_start[0], par])
    spread = call(spread_kernel, 1, 0, [(128, 1280)], [], 8, BF16)(place)
    den = call(denominator_kernel, 3, 1, [(5, 3, 1152)], [])(
        place, occupied_energy, virtual_energy, virtual_energy.reshape(1, 192)
    )
    new, inc = call(
        final_kernel, 1, 4, [(5, 3, 1152)] * 2, [pltpu.VMEM((192, 128), F32), pltpu.VMEM((3, 1152), F32)]
    )(place, got, spread, den, res)
    return jnp.transpose(new, (1, 0, 2)), jnp.transpose(inc, (1, 0, 2))


def solution(mesh):
    fine = Mesh(mesh.devices.reshape(SIZES), AXES)
    split = P(("x", "y", "zh", "core"), ("pair", "par"), None)
    return jax.shard_map(
        body, mesh=fine, in_specs=(split, split, split, P(), P(), P()), out_specs=(split, split), check_vma=False
    )
```

```python
import jax
import jax.numpy as jnp
from jax import lax
from jax.experimental import pallas as pl
from jax.experimental.pallas import tpu as pltpu
from jax.sharding import Mesh, PartitionSpec as P

AXES = ("x", "y", "zh", "core", "pair", "par")
SIZES = (4, 4, 2, 2, 4, 2)
F32, BF16 = jnp.float32, jnp.bfloat16
VMEM = pl.BlockSpec(memory_space=pltpu.VMEM)
SMEM = pl.BlockSpec(memory_space=pltpu.SMEM)
NT = (((1,), (1,)), ((), ()))
NN = (((1,), (0,)), ((), ()))


def index(shape, axis):
    return lax.broadcasted_iota(jnp.int32, shape, axis)


def third(n, count):
    return sum((n >= 3 * s).astype(jnp.int32) for s in range(1, count))


def hot(mask):
    return jnp.where(mask, 1.0, 0.0).astype(BF16)


def order_matrix(e):
    n = index((1, 384), 1)
    source = (n * 10923) >> 16
    m = n - source * 6 - e * 3
    v = ((source >> 2) & 3) * 48 + (source >> 4) * 12 + ((source >> 1) & 1) * 6 + (source & 1) * 3 + m
    v = jnp.where((m >= 0) & (m < 3), v, -1)
    return hot(index((256, 384), 0) == v)


def choose_matrix():
    n = index((1, 256), 1)
    block = sum((n >= 24 * s).astype(jnp.int32) for s in range(1, 11))
    q = n - block * 24
    yz = third(q, 8)
    v = (block >> 1) * 48 + (block & 1) * 3 + yz * 6 + q - yz * 3
    v = jnp.where(block < 8, v, -1)
    return hot(index((256, 256), 0) == v)


def turn_matrix():
    n = index((1, 384), 1)
    p, q = n >> 7, n & 127
    k = sum((q >= 24 * s).astype(jnp.int32) for s in range(1, 6))
    q = q - k * 24
    yz = third(q, 8)
    row = k * 96 + (yz >> 1) * 24 + (yz & 1) * 9 + p * 3 + q - yz * 3
    row = jnp.where(k < 5, row, -1)
    return hot(index((480, 384), 0) == row)


def spread_matrix(par):
    n = index((1, 1280), 1)
    j, q = n >> 8, n & 255
    slot = jnp.where((j & 1) == par, (j - par) >> 1, (j >> 1) + 3 - par)
    x = sum((q >= 48 * s).astype(jnp.int32) for s in range(1, 6))
    q = q - x * 48
    core = third(q, 2)
    row = (x * 2 + core) * 16 + slot * 3 + q - core * 3
    row = jnp.where((x < 4) & (q < 6), row, -1)
    return hot(index((128, 1280), 0) == row)


def dot(a, b, dims=NN):
    return lax.dot_general(a, b, dims, preferred_element_type=F32)


def split2(v):
    high = v.astype(BF16)
    return high, (v - high.astype(F32)).astype(BF16)


def moved(v, hot):
    high = v.astype(BF16)
    rest = v - high.astype(F32)
    mid = rest.astype(BF16)
    low = (rest - mid.astype(F32)).astype(BF16)
    return (dot(low, hot) + dot(mid, hot)) + dot(high, hot)


def weights_kernel(ints_ref, token_ref, out_ref):
    out_ref[...] = jnp.zeros_like(out_ref)
    for k in range(5):
        for n in range(20):
            at = n // 5 * 16 + n % 5 * 3
            out_ref[k, at:at + 3, :] = ints_ref[k, :, n * 384:(n + 1) * 384]


def swap_kernel(own_ref, two_ref, rows):
    rows[...] = jnp.zeros_like(rows)
    for k in range(5):
        for p in range(3):
            v = own_ref[k, :, p * 384:(p + 1) * 384]
            at = k * 24 + p * 6
            rows[at:at + 3, :] = v[:, :256]
            rows[at + 3:at + 6, :] = pltpu.roll(v[:, 128:], 192, 1)
    chosen = moved(rows[...], choose_matrix())
    lane = index((24, 128), 1)
    for n in range(8):
        part = jnp.zeros((24, 128), F32)
        for k in range(5):
            v = pltpu.roll(chosen[k * 24:(k + 1) * 24, :], (k * 24 - n * 24) % 256, 1)[:, :128]
            part = jnp.where((lane >= k * 24) & (lane < k * 24 + 24), v, part)
        for zh in range(2):
            at = (n // 2 * 4 + zh * 2 + n % 2) * 18
            two_ref[at:at + 18, :] = part[:18]


def merge_kernel(zh_ref, own_ref, other_ref, out_ref, rows):
    first = zh_ref[0] == 0
    rows[...] = jnp.zeros_like(rows)
    for k in range(5):
        for p in range(3):
            own = own_ref[k, :, p * 384:(p + 1) * 384]
            other = other_ref[k, :, p * 384:(p + 1) * 384]
            at = k * 18 + p * 3
            rows[at:at + 3, :] = jnp.where(first, own, other)
            rows[at + 9:at + 12, :] = jnp.where(first, other, own)
    for part in range(3):
        out_ref[part * 96:(part + 1) * 96, :] = rows[:, part * 128:(part + 1) * 128]


def pack_kernel(one_ref, two_ref, out_ref):
    for y in range(4):
        out_ref[y, :288, :] = one_ref[...]
        out_ref[y, 288:, :] = two_ref[...]


def mark_kernel(*refs):
    refs[-1][...] = jnp.zeros_like(refs[-1])


def product_kernel(par_ref, got_ref, *refs):
    weights, (keep_ref, send_ref) = refs[:8], refs[10:12]
    two_high, two_low, stage, swapped, whole, mixed = refs[12:]
    for p in range(3):
        for y in range(4):
            for n in range(16):
                at = 288 + n * 18 + p * 6
                stage[y * 96 + n * 6:y * 96 + n * 6 + 6, :] = got_ref[y, at:at + 6, :]
        high, low = split2(stage[...])
        two_high[:, p * 128:(p + 1) * 128] = high
        two_low[:, p * 128:(p + 1) * 128] = low
    turn = turn_matrix()
    parts = [dot(turn, two[...], NT).astype(BF16) for two in (two_high, two_low)]
    parts = jnp.concatenate(parts, 0)
    for e in range(2):
        moved_parts = dot(parts, order_matrix(e), NT)
        swapped[e] = moved_parts[:480] + moved_parts[480:]
    lane = index((24, 256), 1)
    for k in range(5):
        for y in range(4):
            v = [got_ref[y, part * 96 + k * 18:part * 96 + k * 18 + 24, :] for part in range(3)]
            near = jnp.concatenate(v[:2], 1)
            far = pltpu.roll(jnp.concatenate(v[1:], 1), 192, 1)
            for e, straight in enumerate((near, far)):
                at = (k * 4 + y) * 24
                value = 2.0 * jnp.where(lane < 192, straight, 0.0) - swapped[e, at:at + 24, :]
                whole[y * 48 + e * 24:y * 48 + e * 24 + 24, :] = value
        high, low = split2(whole[...])
        mixed[k, :192] = high
        mixed[k, 192:] = low
    even = par_ref[0] == 0
    slot = index((192, 128), 1) & 15
    for q in range(4):
        total = jnp.zeros((192, 256), F32)
        for k in range(5):
            rows = [ref[k, q * 16:(q + 1) * 16, :] for ref in weights]
            near = [v[:, :256] for v in rows]
            far = [pltpu.roll(v[:, 128:], 192, 1) for v in rows]
            high, low = split2(jnp.concatenate(near + far, 0))
            both = dot(mixed[k], high, NT)
            total += dot(mixed[k, :192], low, NT) + both[192:]
            total += both[:192]
        near, far = total[:, :128], total[:, 128:]
        first = jnp.where(slot < 9, near, pltpu.roll(far, 9, 1))
        second = jnp.where(slot < 6, pltpu.roll(near, 119, 1), far)
        for ref, v in ((keep_ref, jnp.where(even, first, second)), (send_ref, jnp.where(even, second, first))):
            for yz in range(8):
                for e in range(2):
                    to = (yz * 4 + q) * 18 + e * 9
                    at = yz // 2 * 48 + e * 24 + yz % 2 * 9
                    ref[to:to + 9, :] = v[at:at + 9, :]


def spread_kernel(place_ref, out_ref):
    out_ref[...] = spread_matrix(place_ref[5])


def denominator_kernel(place_ref, occ_ref, va_ref, vb_ref, out_ref):
    row = index((3, 192), 0)
    va = [va_ref[place_ref[2] + m] for m in range(3)]
    va = jnp.where(row == 0, va[0], jnp.where(row == 1, va[1], va[2]))
    base = vb_ref[...] + va
    for j in range(5):
        for i in range(6):
            out_ref[j, :, i * 192:(i + 1) * 192] = base - occ_ref[place_ref[4] + i] - occ_ref[place_ref[3] + j]


def final_kernel(place_ref, got_ref, spread_ref, den_ref, res_ref, new_ref, inc_ref, sums, cyc):
    sums[...] = jnp.zeros_like(sums)
    for yz in range(8):
        total = got_ref[yz * 72:yz * 72 + 18, :]
        for z in range(1, 4):
            at = (yz * 4 + z) * 18
            total += got_ref[at:at + 18, :]
        sums[yz * 24:yz * 24 + 18, :] = total
    v = pltpu.roll(sums[...], place_ref[0] * 32, 1)
    lane = index(v.shape, 1)
    other = jnp.where((lane & 16) == 0, pltpu.roll(v, 112, 1), pltpu.roll(v, 16, 1))
    v = jnp.where(place_ref[1] == 0, v, other)
    wide = moved(v, spread_ref[...])
    for j in range(5):
        total = wide[0:24, j * 256:(j + 1) * 256]
        for yz in range(1, 8):
            total += pltpu.roll(wide[yz * 24:(yz + 1) * 24, j * 256:(j + 1) * 256], yz * 6, 1)
        for i in range(6):
            at = i % 2 * 9 + i // 2 * 3
            cyc[:, i * 192:(i + 1) * 192] = total[at:at + 3, :192]
        new = res_ref[j] + cyc[...]
        new_ref[j] = new
        inc_ref[j] = new / den_ref[j]


def call(kernel, n_smem, n_vmem, outs, scratch, mib=8, dtype=F32, cost=1000, space=pltpu.VMEM):
    shapes = [jax.ShapeDtypeStruct(s, dtype) for s in outs]
    return pl.pallas_call(
        kernel,
        out_shape=shapes if len(shapes) > 1 else shapes[0],
        in_specs=[SMEM] * n_smem + [pl.BlockSpec(memory_space=space)] * n_vmem,
        out_specs=[VMEM] * len(shapes) if len(shapes) > 1 else VMEM,
        scratch_shapes=scratch,
        cost_estimate=pl.CostEstimate(flops=cost * 10**6, bytes_accessed=1000, transcendentals=0),
        compiler_params=pltpu.CompilerParams(vmem_limit_bytes=mib * 1024 * 1024),
    )


def body(amplitudes, integrals, residual, occupied_energy, virtual_energy, window_start):
    x, y, zh, core, pair, par = [lax.axis_index(a).astype(jnp.int32) for a in AXES]
    amps = jnp.transpose(amplitudes, (1, 0, 2))
    ints = jnp.transpose(integrals, (1, 0, 2))
    res = jnp.transpose(residual, (1, 0, 2))
    other = lax.ppermute(amps, "zh", [(0, 1), (1, 0)])
    two = call(swap_kernel, 0, 1, [(288, 128)], [pltpu.VMEM((120, 256), F32)])(amps)
    weights = call(weights_kernel, 0, 2, [(5, 64, 384)], [])(ints, other)
    along = [weights] + [
        lax.ppermute(weights, "x", [(s, (s - d) % 4) for s in range(4)]) for d in (1, 3, 2)
    ]
    across = [lax.ppermute(w, "core", [(0, 1), (1, 0)]) for w in along]
    two = lax.all_to_all(two.reshape(16, 1, 2304), ("x", "zh", "core"), 0, 0, tiled=True).reshape(288, 128)
    one = call(merge_kernel, 1, 2, [(288, 128)], [pltpu.VMEM((96, 384), F32)], cost=8000)(zh.reshape(1), amps, other)
    both = call(pack_kernel, 0, 2, [(4, 576, 128)], [])(one, two)
    both = lax.all_to_all(both, "y", 0, 0, tiled=True)
    ordered = [w for pair in zip(along, across) for w in pair]
    ordered = ordered[:4] + ordered[6:] + ordered[4:6]
    mark = call(mark_kernel, 0, 4, [(8, 128)], [], 8, F32, 5000, pl.ANY)(*along)
    wait = call(mark_kernel, 0, 1, [(8, 128)], [], 8, F32, 1000, pl.ANY)(both)
    keep, send = pl.pallas_call(
        product_kernel,
        out_shape=[jax.ShapeDtypeStruct((576, 128), F32)] * 2,
        in_specs=[SMEM] + [VMEM] * 9 + [pl.BlockSpec(memory_space=pl.ANY)] * 2,
        out_specs=[VMEM] * 2,
        scratch_shapes=[pltpu.VMEM((384, 384), BF16)] * 2 + [pltpu.VMEM((384, 128), F32)]
        + [pltpu.VMEM((2, 480, 256), F32), pltpu.VMEM((192, 256), F32), pltpu.VMEM((5, 384, 256), BF16)],
        cost_estimate=pl.CostEstimate(flops=10**9, bytes_accessed=1000, transcendentals=0),
        compiler_params=pltpu.CompilerParams(vmem_limit_bytes=24 * 1024 * 1024),
    )(par.reshape(1), both, *ordered, mark, wait)
    half = keep + lax.ppermute(send, "par", [(0, 1), (1, 0)])
    got = lax.all_to_all(half.reshape(32, 1, 2304), ("y", "zh", "pair"), 0, 0, tiled=True).reshape(576, 128)
    r = ((x * 4 + y) * 2 + zh) * 2 + core
    place = jnp.stack([x, core, r * 3, (pair * 2 + par) * 5, window_start[0], par])
    spread = call(spread_kernel, 1, 0, [(128, 1280)], [], 8, BF16)(place)
    den = call(denominator_kernel, 3, 1, [(5, 3, 1152)], [])(
        place, occupied_energy, virtual_energy, virtual_energy.reshape(1, 192)
    )
    new, inc = call(
        final_kernel, 1, 4, [(5, 3, 1152)] * 2, [pltpu.VMEM((192, 128), F32), pltpu.VMEM((3, 1152), F32)]
    )(place, got, spread, den, res)
    return jnp.transpose(new, (1, 0, 2)), jnp.transpose(inc, (1, 0, 2))


def solution(mesh):
    fine = Mesh(mesh.devices.reshape(SIZES), AXES)
    split = P(("x", "y", "zh", "core"), ("pair", "par"), None)
    return jax.shard_map(
        body, mesh=fine, in_specs=(split, split, split, P(), P(), P()), out_specs=(split, split), check_vma=False
    )
```

```python
import jax
import jax.numpy as jnp
from jax import lax
from jax.experimental import pallas as pl
from jax.experimental.pallas import tpu as pltpu
from jax.sharding import Mesh, PartitionSpec as P

AXES = ("x", "y", "zh", "core", "pair", "par")
SIZES = (4, 4, 2, 2, 4, 2)
F32, BF16 = jnp.float32, jnp.bfloat16
VMEM = pl.BlockSpec(memory_space=pltpu.VMEM)
SMEM = pl.BlockSpec(memory_space=pltpu.SMEM)
NT = (((1,), (1,)), ((), ()))
NN = (((1,), (0,)), ((), ()))


def index(shape, axis):
    return lax.broadcasted_iota(jnp.int32, shape, axis)


def third(n, count):
    return sum((n >= 3 * s).astype(jnp.int32) for s in range(1, count))


def hot(mask):
    return jnp.where(mask, 1.0, 0.0).astype(BF16)


def order_matrix(e):
    n = index((1, 384), 1)
    source = (n * 10923) >> 16
    m = n - source * 6 - e * 3
    v = ((source >> 2) & 3) * 48 + (source >> 4) * 12 + ((source >> 1) & 1) * 6 + (source & 1) * 3 + m
    v = jnp.where((m >= 0) & (m < 3), v, -1)
    return hot(index((256, 384), 0) == v)


def choose_matrix():
    n = index((1, 256), 1)
    block = sum((n >= 24 * s).astype(jnp.int32) for s in range(1, 11))
    q = n - block * 24
    yz = third(q, 8)
    v = (block >> 1) * 48 + (block & 1) * 3 + yz * 6 + q - yz * 3
    v = jnp.where(block < 8, v, -1)
    return hot(index((256, 256), 0) == v)


def turn_matrix():
    n = index((1, 384), 1)
    p, q = n >> 7, n & 127
    k = sum((q >= 24 * s).astype(jnp.int32) for s in range(1, 6))
    q = q - k * 24
    yz = third(q, 8)
    row = k * 96 + (yz >> 1) * 24 + (yz & 1) * 9 + p * 3 + q - yz * 3
    row = jnp.where(k < 5, row, -1)
    return hot(index((480, 384), 0) == row)


def spread_matrix(par):
    n = index((1, 1280), 1)
    j, q = n >> 8, n & 255
    slot = jnp.where((j & 1) == par, (j - par) >> 1, (j >> 1) + 3 - par)
    x = sum((q >= 48 * s).astype(jnp.int32) for s in range(1, 6))
    q = q - x * 48
    core = third(q, 2)
    row = (x * 2 + core) * 16 + slot * 3 + q - core * 3
    row = jnp.where((x < 4) & (q < 6), row, -1)
    return hot(index((128, 1280), 0) == row)


def dot(a, b, dims=NN):
    return lax.dot_general(a, b, dims, preferred_element_type=F32)


def split2(v):
    high = v.astype(BF16)
    return high, (v - high.astype(F32)).astype(BF16)


def moved(v, hot):
    high = v.astype(BF16)
    rest = v - high.astype(F32)
    mid = rest.astype(BF16)
    low = (rest - mid.astype(F32)).astype(BF16)
    return (dot(low, hot) + dot(mid, hot)) + dot(high, hot)


def weights_kernel(ints_ref, token_ref, out_ref):
    out_ref[...] = jnp.zeros_like(out_ref)
    for k in range(5):
        for n in range(20):
            at = n // 5 * 16 + n % 5 * 3
            out_ref[k, at:at + 3, :] = ints_ref[k, :, n * 384:(n + 1) * 384]


def swap_kernel(own_ref, two_ref, rows):
    rows[...] = jnp.zeros_like(rows)
    for k in range(5):
        for p in range(3):
            v = own_ref[k, :, p * 384:(p + 1) * 384]
            at = k * 24 + p * 6
            rows[at:at + 3, :] = v[:, :256]
            rows[at + 3:at + 6, :] = pltpu.roll(v[:, 128:], 192, 1)
    chosen = moved(rows[...], choose_matrix())
    lane = index((24, 128), 1)
    for n in range(8):
        part = jnp.zeros((24, 128), F32)
        for k in range(5):
            v = pltpu.roll(chosen[k * 24:(k + 1) * 24, :], (k * 24 - n * 24) % 256, 1)[:, :128]
            part = jnp.where((lane >= k * 24) & (lane < k * 24 + 24), v, part)
        for zh in range(2):
            at = (n // 2 * 4 + zh * 2 + n % 2) * 18
            two_ref[at:at + 18, :] = part[:18]


def merge_kernel(zh_ref, own_ref, other_ref, out_ref, rows):
    first = zh_ref[0] == 0
    rows[...] = jnp.zeros_like(rows)
    for k in range(5):
        for p in range(3):
            own = own_ref[k, :, p * 384:(p + 1) * 384]
            other = other_ref[k, :, p * 384:(p + 1) * 384]
            at = k * 18 + p * 3
            rows[at:at + 3, :] = jnp.where(first, own, other)
            rows[at + 9:at + 12, :] = jnp.where(first, other, own)
    for part in range(3):
        out_ref[part * 96:(part + 1) * 96, :] = rows[:, part * 128:(part + 1) * 128]


def pack_kernel(one_ref, two_ref, out_ref):
    for y in range(4):
        out_ref[y, :288, :] = one_ref[...]
        out_ref[y, 288:, :] = two_ref[...]


def mark_kernel(*refs):
    refs[-1][...] = jnp.zeros_like(refs[-1])


def product_kernel(par_ref, got_ref, *refs):
    weights, (keep_ref, send_ref) = refs[:8], refs[10:12]
    two_high, two_low, stage, swapped, whole, mixed = refs[12:]
    for p in range(3):
        for y in range(4):
            for n in range(16):
                at = 288 + n * 18 + p * 6
                stage[y * 96 + n * 6:y * 96 + n * 6 + 6, :] = got_ref[y, at:at + 6, :]
        high, low = split2(stage[...])
        two_high[:, p * 128:(p + 1) * 128] = high
        two_low[:, p * 128:(p + 1) * 128] = low
    turn = turn_matrix()
    parts = [dot(turn, two[...], NT).astype(BF16) for two in (two_high, two_low)]
    parts = jnp.concatenate(parts, 0)
    for e in range(2):
        moved_parts = dot(parts, order_matrix(e), NT)
        swapped[e] = moved_parts[:480] + moved_parts[480:]
    lane = index((24, 256), 1)
    for k in range(5):
        for y in range(4):
            v = [got_ref[y, part * 96 + k * 18:part * 96 + k * 18 + 24, :] for part in range(3)]
            near = jnp.concatenate(v[:2], 1)
            far = pltpu.roll(jnp.concatenate(v[1:], 1), 192, 1)
            for e, straight in enumerate((near, far)):
                at = (k * 4 + y) * 24
                value = 2.0 * jnp.where(lane < 192, straight, 0.0) - swapped[e, at:at + 24, :]
                whole[y * 48 + e * 24:y * 48 + e * 24 + 24, :] = value
        high, low = split2(whole[...])
        mixed[k, :192] = high
        mixed[k, 192:] = low
    even = par_ref[0] == 0
    slot = index((192, 128), 1) & 15
    for q in range(4):
        total = jnp.zeros((192, 256), F32)
        for k in range(5):
            rows = [ref[k, q * 16:(q + 1) * 16, :] for ref in weights]
            near = [v[:, :256] for v in rows]
            far = [pltpu.roll(v[:, 128:], 192, 1) for v in rows]
            high, low = split2(jnp.concatenate(near + far, 0))
            both = dot(mixed[k], high, NT)
            total += dot(mixed[k, :192], low, NT) + both[192:]
            total += both[:192]
        near, far = total[:, :128], total[:, 128:]
        first = jnp.where(slot < 9, near, pltpu.roll(far, 9, 1))
        second = jnp.where(slot < 6, pltpu.roll(near, 119, 1), far)
        for ref, v in ((keep_ref, jnp.where(even, first, second)), (send_ref, jnp.where(even, second, first))):
            for yz in range(8):
                for e in range(2):
                    to = (yz * 4 + q) * 18 + e * 9
                    at = yz // 2 * 48 + e * 24 + yz % 2 * 9
                    ref[to:to + 9, :] = v[at:at + 9, :]


def spread_kernel(place_ref, out_ref):
    out_ref[...] = spread_matrix(place_ref[5])


def denominator_kernel(place_ref, occ_ref, va_ref, vb_ref, out_ref):
    row = index((3, 192), 0)
    va = [va_ref[place_ref[2] + m] for m in range(3)]
    va = jnp.where(row == 0, va[0], jnp.where(row == 1, va[1], va[2]))
    base = vb_ref[...] + va
    for j in range(5):
        for i in range(6):
            out_ref[j, :, i * 192:(i + 1) * 192] = base - occ_ref[place_ref[4] + i] - occ_ref[place_ref[3] + j]


def final_kernel(place_ref, got_ref, spread_ref, den_ref, res_ref, new_ref, inc_ref, sums, cyc):
    sums[...] = jnp.zeros_like(sums)
    for yz in range(8):
        total = got_ref[yz * 72:yz * 72 + 18, :]
        for z in range(1, 4):
            at = (yz * 4 + z) * 18
            total += got_ref[at:at + 18, :]
        sums[yz * 24:yz * 24 + 18, :] = total
    v = pltpu.roll(sums[...], place_ref[0] * 32, 1)
    lane = index(v.shape, 1)
    other = jnp.where((lane & 16) == 0, pltpu.roll(v, 112, 1), pltpu.roll(v, 16, 1))
    v = jnp.where(place_ref[1] == 0, v, other)
    wide = moved(v, spread_ref[...])
    for j in range(5):
        total = wide[0:24, j * 256:(j + 1) * 256]
        for yz in range(1, 8):
            total += pltpu.roll(wide[yz * 24:(yz + 1) * 24, j * 256:(j + 1) * 256], yz * 6, 1)
        for i in range(6):
            at = i % 2 * 9 + i // 2 * 3
            cyc[:, i * 192:(i + 1) * 192] = total[at:at + 3, :192]
        new = res_ref[j] + cyc[...]
        new_ref[j] = new
        inc_ref[j] = new / den_ref[j]


def call(kernel, n_smem, n_vmem, outs, scratch, mib=8, dtype=F32, cost=1000, space=pltpu.VMEM):
    shapes = [jax.ShapeDtypeStruct(s, dtype) for s in outs]
    return pl.pallas_call(
        kernel,
        out_shape=shapes if len(shapes) > 1 else shapes[0],
        in_specs=[SMEM] * n_smem + [pl.BlockSpec(memory_space=space)] * n_vmem,
        out_specs=[VMEM] * len(shapes) if len(shapes) > 1 else VMEM,
        scratch_shapes=scratch,
        cost_estimate=pl.CostEstimate(flops=cost * 10**6, bytes_accessed=1000, transcendentals=0),
        compiler_params=pltpu.CompilerParams(vmem_limit_bytes=mib * 1024 * 1024),
    )


def body(amplitudes, integrals, residual, occupied_energy, virtual_energy, window_start):
    x, y, zh, core, pair, par = [lax.axis_index(a).astype(jnp.int32) for a in AXES]
    amps = jnp.transpose(amplitudes, (1, 0, 2))
    ints = jnp.transpose(integrals, (1, 0, 2))
    res = jnp.transpose(residual, (1, 0, 2))
    other = lax.ppermute(amps, "zh", [(0, 1), (1, 0)])
    two = call(swap_kernel, 0, 1, [(288, 128)], [pltpu.VMEM((120, 256), F32)])(amps)
    weights = call(weights_kernel, 0, 2, [(5, 64, 384)], [])(ints, other)
    near, back = [lax.ppermute(weights, "x", [(s, (s - d) % 4) for s in range(4)]) for d in (1, 3)]
    along = [weights, near, back, lax.ppermute(near, "x", [(s, (s - 1) % 4) for s in range(4)])]
    across = [lax.ppermute(w, "core", [(0, 1), (1, 0)]) for w in along]
    two = lax.all_to_all(two.reshape(16, 1, 2304), ("x", "zh", "core"), 0, 0, tiled=True).reshape(288, 128)
    one = call(merge_kernel, 1, 2, [(288, 128)], [pltpu.VMEM((96, 384), F32)], cost=8000)(zh.reshape(1), amps, other)
    both = call(pack_kernel, 0, 2, [(4, 576, 128)], [])(one, two)
    both = lax.all_to_all(both, "y", 0, 0, tiled=True)
    ordered = [w for pair in zip(along, across) for w in pair]
    ordered = ordered[:4] + ordered[6:] + ordered[4:6]
    mark = call(mark_kernel, 0, 4, [(8, 128)], [], 8, F32, 5000, pl.ANY)(*along)
    wait = call(mark_kernel, 0, 1, [(8, 128)], [], 8, F32, 1000, pl.ANY)(both)
    keep, send = pl.pallas_call(
        product_kernel,
        out_shape=[jax.ShapeDtypeStruct((576, 128), F32)] * 2,
        in_specs=[SMEM] + [VMEM] * 9 + [pl.BlockSpec(memory_space=pl.ANY)] * 2,
        out_specs=[VMEM] * 2,
        scratch_shapes=[pltpu.VMEM((384, 384), BF16)] * 2 + [pltpu.VMEM((384, 128), F32)]
        + [pltpu.VMEM((2, 480, 256), F32), pltpu.VMEM((192, 256), F32), pltpu.VMEM((5, 384, 256), BF16)],
        cost_estimate=pl.CostEstimate(flops=10**9, bytes_accessed=1000, transcendentals=0),
        compiler_params=pltpu.CompilerParams(vmem_limit_bytes=24 * 1024 * 1024),
    )(par.reshape(1), both, *ordered, mark, wait)
    half = keep + lax.ppermute(send, "par", [(0, 1), (1, 0)])
    got = lax.all_to_all(half.reshape(32, 1, 2304), ("y", "zh", "pair"), 0, 0, tiled=True).reshape(576, 128)
    r = ((x * 4 + y) * 2 + zh) * 2 + core
    place = jnp.stack([x, core, r * 3, (pair * 2 + par) * 5, window_start[0], par])
    spread = call(spread_kernel, 1, 0, [(128, 1280)], [], 8, BF16)(place)
    den = call(denominator_kernel, 3, 1, [(5, 3, 1152)], [])(
        place, occupied_energy, virtual_energy, virtual_energy.reshape(1, 192)
    )
    new, inc = call(
        final_kernel, 1, 4, [(5, 3, 1152)] * 2, [pltpu.VMEM((192, 128), F32), pltpu.VMEM((3, 1152), F32)]
    )(place, got, spread, den, res)
    return jnp.transpose(new, (1, 0, 2)), jnp.transpose(inc, (1, 0, 2))


def solution(mesh):
    fine = Mesh(mesh.devices.reshape(SIZES), AXES)
    split = P(("x", "y", "zh", "core"), ("pair", "par"), None)
    return jax.shard_map(
        body, mesh=fine, in_specs=(split, split, split, P(), P(), P()), out_specs=(split, split), check_vma=False
    )
```
